32 devices in a mesh: ex: 8 (over z, x), rep: 4 (over y, core).
Axes of the slice: x: 2, y: 2, z: 4, core: 2. Of those that a mesh axis runs over, the one named last changes fastest.
Arguments:
- tokens: bfloat16 [20480, 1024], P(('ex', 'rep')), may hold values from -6 to 6
- lengths: int32 [10], replicated, may hold values from 1 to 2048, 14336 in all
- assign: int32 [20480, 1], P(('ex', 'rep')), may hold values from 0 to 7; in each aligned block of 640 rows (0 to 639, 640 to 1279, ...) at most 100 rows name the same one
- centroids: bfloat16 [8, 1024], P('ex', 'rep'), may hold values from -0.125 to 0.125
- ln_gain: bfloat16 [8, 2, 1024], P('ex', None, 'rep'), may hold values from 0.5 to 1.5
- ln_bias: bfloat16 [8, 2, 1024], P('ex', None, 'rep'), may hold values from -0.59765625 to 0.59765625
- w_in: bfloat16 [8, 2, 1024, 4096], P('ex', None, None, 'rep'), may hold values from -0.1875 to 0.1875
- b_in: bfloat16 [8, 2, 4096], P('ex', None, 'rep'), may hold values from -0.59765625 to 0.59765625
- w_out: bfloat16 [8, 2, 4096, 1024], P('ex', None, 'rep'), may hold values from -0.09375 to 0.09375
- b_out: bfloat16 [8, 2, 1024], P('ex', None, 'rep'), may hold values from -0.59765625 to 0.59765625
- grad_output: bfloat16 [20480, 1024], P(('ex', 'rep')), may hold values from -6 to 6
Outputs:
- output: bfloat16 [20480, 1024], P(('ex', 'rep'))
- grad_input: bfloat16 [20480, 1024], P(('ex', 'rep'))
- grad_centroids: float32 [8, 1024], P('ex', 'rep')
- grad_ln_gain: float32 [8, 2, 1024], P('ex', None, 'rep')
- grad_ln_bias: float32 [8, 2, 1024], P('ex', None, 'rep')
- grad_w_in: float32 [8, 2, 1024, 4096], P('ex', None, None, 'rep')
- grad_b_in: float32 [8, 2, 4096], P('ex', None, 'rep')
- grad_w_out: float32 [8, 2, 4096, 1024], P('ex', None, 'rep')
- grad_b_out: float32 [8, 2, 1024], P('ex', None, 'rep')
The draws below stay inside these ranges and needn't reach their ends.
Inputs may be any that keep to these rules, and one draw needn't show every extreme that they name: `assign`: in the rows of one device no expert is named by more than 100 rows, a bound that some block reaches; padding rows carry an expert too but are ignored. Sequence s holds rows s * 2048 to (s + 1) * 2048 - 1, of which the first lengths[s] are tokens and the rest padding; the lengths sum to 14336 and the largest is 2048.
All inputs are finite; a program needn't handle non-finite values.
Results may differ from the reference program's by a relative error of at most 0.011.
Values may be sent and summed in bfloat16 or wider, within the bound.
No kernel may reach another device: no remote copies, remote signals or barrier semaphores. Data moves between devices by JAX's collectives and lax.ppermute only.
A program may use at most 256 MiB of HBM per device.

```python
import math
import jax
import jax.numpy as jnp
import numpy as np
from jax import lax

D = 1024
FF = 4096
EXPERTS = 8
TOK_DEV = 640
SEQ_LEN = 2048
TOKENS = 20480
NSEQ = 10
REAL = 14336
MOST = 100
N_EX = 8
N_REP = 4


def steps_of(stream_key, extent, split, smallest, top_value):
    gain = 1.0
    for dim, blocks in split:
        heights = jax.random.uniform(jax.random.fold_in(jax.random.fold_in(stream_key, 6), dim), (blocks,), jnp.float32, smallest / len(split), top_value / len(split))
        gain = gain * jnp.repeat(jnp.exp(heights), extent[dim] // blocks).reshape((-1,) + (1,) * (len(extent) - 1 - dim))
    return gain


def length_profile(count, total, reach, lean):
    weights = [(1 << 20) // math.isqrt(standing ** lean) + 1 for standing in range(2, count + 1)]
    spare, given = total - reach - (count - 1), [1] * (count - 1)
    while spare > 0:
        free = [i for i in range(count - 1) if given[i] < reach]
        pool, left = sum([weights[i] for i in free]), spare
        for i in free:
            extra = min(reach - given[i], max(1, left * weights[i] // pool), spare)
            given[i] = given[i] + extra
            spare = spare - extra
    return np.array([reach] + given)


def ragged(rng, amount, total, limit, slope):
    if amount == 2:
        one = jax.random.randint(rng, (), max(1, total - limit), min(limit, total - 1) + 1)
        return jnp.stack([one, total - one])
    sizes = jnp.asarray(length_profile(amount, total, limit, slope), jnp.int32)
    pairs = (amount - 1) // 2
    source_of, taker = sizes[1:1 + 2 * pairs:2], sizes[2:2 + 2 * pairs:2]
    margin = jnp.minimum(source_of - 1, limit - taker)
    moved = jax.random.randint(jax.random.fold_in(rng, 1), (pairs,), 0, 1 << 20) % (margin + 1)
    sizes = sizes.at[1:1 + 2 * pairs:2].set(source_of - moved).at[2:2 + 2 * pairs:2].set(taker + moved)
    return sizes[jax.random.permutation(jax.random.fold_in(rng, 2), amount)]


def shared_out(stream_key, own, number, rows, amount, top, reach, slope):
    ranking = jax.random.permutation(stream_key, amount)
    heavy_load, common = shares(amount, rows * top, reach, slope, True), shares(amount, rows * top, reach, slope, False)
    places = jnp.arange(amount)

    def named(sizes, rotation):
        used = int((sizes > 0).sum())
        fixed = max(1, used // 4)
        shifted = fixed + (places - fixed + rotation * (used - fixed)) % max(1, amount - fixed)
        return jnp.zeros((amount,), jnp.int32).at[ranking[jnp.where(places < fixed, places, shifted)]].set(jnp.asarray(sizes, jnp.int32))

    sizes = jnp.where(number % 4 == 0, named(heavy_load, number // 4), named(common, number - number // 4 - 1))
    mixed = jax.random.permutation(jax.random.fold_in(own, 3), amount)
    source_of, taker = mixed[0:amount // 2 * 2:2], mixed[1:amount // 2 * 2:2]
    room = jnp.minimum(sizes[source_of] - 1, reach - sizes[taker]) // 2
    room = jnp.where((source_of == ranking[0]) | (taker == ranking[0]) | (sizes[taker] == 0), 0, jnp.maximum(room, 0))
    shifted = jax.random.randint(jax.random.fold_in(own, 4), (amount // 2,), 0, 1 << 20) % (room + 1)
    sizes = sizes.at[source_of].add(-shifted).at[taker].add(shifted)
    items = jnp.searchsorted(jnp.cumsum(sizes), jnp.arange(rows * top), side="right").astype(jnp.int32)
    table = items.reshape(top, rows).T
    table = table[jax.random.permutation(jax.random.fold_in(own, 1), rows)]
    rotation = jax.random.randint(jax.random.fold_in(own, 2), (rows, 1), 0, top)
    return jnp.take_along_axis(table, (jnp.arange(top)[None, :] + rotation) % top, axis=1)


def shares(count, total, reach, lean, full):
    loads = [(1 << 20) // math.isqrt(grade ** lean) + 1 for grade in range(1, count + 1)]
    largest = reach if full else min(reach, max(-(-total // count), total * loads[0] // sum(loads)))
    least = 1 if total - largest >= count - 1 else 0
    counts, spare = [largest] + [least] * (count - 1), total - largest - least * (count - 1)
    while spare > 0:
        movable = [i for i in range(1, count) if counts[i] < largest] or [i for i in range(1, count) if counts[i] < reach]
        pool, remaining = sum([loads[i] for i in movable]), spare
        for i in movable:
            more = min(reach - counts[i], max(1, remaining * loads[i] // pool), spare)
            counts[i] = counts[i] + more
            spare = spare - more
    return np.array(counts)


def normal_values(own_key, shape, width, bound, pieces=(), kind=jnp.bfloat16):
    gain = steps_of(own_key, shape, pieces, -0.22, 0.18) if pieces else 1.0
    values = jax.random.normal(own_key, shape, jnp.float32) * width * gain
    return jnp.minimum(jnp.maximum(values, -bound), bound).astype(kind)


def setup_inputs(seed: int = 0) -> dict:
    streams_of = jax.random.split(jax.random.key(seed), 12)
    tokens = normal_values(streams_of[0], (TOKENS, D), 1.0, 6.0, ((0, 32),))
    lengths = ragged(streams_of[1], NSEQ, REAL, SEQ_LEN, 2).astype(jnp.int32)
    assign_keys = jax.random.split(jax.random.fold_in(streams_of[2], 1), TOKENS // TOK_DEV)
    assign_turns = jax.random.permutation(jax.random.fold_in(streams_of[2], 3), TOKENS // TOK_DEV)
    assign = jax.vmap(lambda own, number: shared_out(jax.random.fold_in(streams_of[2], 2), own, number, TOK_DEV, EXPERTS, 1, MOST, 0))(assign_keys, assign_turns).reshape((TOKENS, 1))
    centroids = normal_values(streams_of[3], (EXPERTS, D), (2 * D) ** -0.5, 0.125, ((0, 8), (1, 4)))
    ln_gain = jnp.clip(1.0 + 0.1 * jax.random.normal(streams_of[4], (EXPERTS, 2, D), jnp.float32), 0.5, 1.5).astype(jnp.bfloat16)
    ln_bias = normal_values(streams_of[5], (EXPERTS, 2, D), 0.1, 0.59765625, ((0, 8), (2, 4)))
    w_in = normal_values(streams_of[6], (EXPERTS, 2, D, FF), D ** -0.5, 0.1875, ((0, 8), (3, 4)))
    b_in = normal_values(streams_of[7], (EXPERTS, 2, FF), 0.1, 0.59765625, ((0, 8), (2, 4)))
    w_out = normal_values(streams_of[8], (EXPERTS, 2, FF, D), FF ** -0.5, 0.09375, ((0, 8), (2, 4)))
    b_out = normal_values(streams_of[9], (EXPERTS, 2, D), 0.1, 0.59765625, ((0, 8), (2, 4)))
    grad_output = normal_values(streams_of[10], (TOKENS, D), 1.0, 6.0, ((0, 32),))
    return dict(tokens=tokens, lengths=lengths, assign=assign, centroids=centroids, ln_gain=ln_gain, ln_bias=ln_bias, w_in=w_in, b_in=b_in, w_out=w_out, b_out=b_out, grad_output=grad_output)


EPSILON = 1e-05
HIGHEST = lax.Precision.HIGHEST

@jax.custom_vjp
def low(v):
    return lax.optimization_barrier(v.astype(jnp.bfloat16)).astype(jnp.float32)

@jax.custom_vjp
def low_back(v):
    return v

def low_keep(v):
    return (low(v), None)

def low_pass(kept, grad):
    return (grad,)

def back_keep(v):
    return (v, None)

def back_low(kept, grad):
    return (low(grad),)
low.defvjp(low_keep, low_pass)
low_back.defvjp(back_keep, back_low)

def layer_norm(hidden, scale_in, shift_in):
    center = hidden - lax.optimization_barrier(jnp.mean(hidden, -1, keepdims=True))
    variance = lax.optimization_barrier(jnp.mean(center * center, -1, keepdims=True))
    return center * lax.rsqrt(variance + EPSILON) * scale_in + shift_in

def expert_rows(operands):
    inputs, centroid, gain_rows, shifts, w_first, b_first, w_second, b_second = operands
    logits = low_back(jnp.dot(inputs, centroid, precision=HIGHEST))
    gating = jax.nn.sigmoid(logits)
    hidden = inputs
    for sublayer in range(2):
        normed = low(layer_norm(hidden, gain_rows[sublayer], shifts[sublayer]))
        preact = low_back(jnp.dot(normed, w_first[sublayer], precision=HIGHEST)) + b_first[sublayer]
        active = low(jax.nn.gelu(preact, approximate=True))
        hidden = hidden + low_back(jnp.dot(active, w_second[sublayer], precision=HIGHEST)) + b_second[sublayer]
    return low(gating[:, None] * hidden)

def reference(tokens, lengths, assign, centroids, ln_gain, ln_bias, w_in, b_in, w_out, b_out, grad_output):
    expert_count = EXPERTS
    capacity = N_EX * N_REP * MOST
    position = jnp.arange(TOKENS, dtype=jnp.int32)
    sequence = (position // SEQ_LEN).astype(jnp.int32)
    live_rows = position % SEQ_LEN < lengths[sequence]
    expert = assign[:, 0].astype(jnp.int32)
    sort_key = jnp.where(live_rows, expert, expert_count).astype(jnp.int32)
    ordering = jnp.argsort(sort_key, stable=True).astype(jnp.int32)
    expert_ids = jnp.arange(expert_count, dtype=jnp.int32)
    expert_loads = lax.optimization_barrier(jnp.sum((sort_key[:, None] == expert_ids[None, :]).astype(jnp.int32), 0)).astype(jnp.int32)
    starts = (jnp.cumsum(expert_loads) - expert_loads).astype(jnp.int32)
    sorted_at = jnp.zeros((TOKENS,), jnp.int32).at[ordering].set(position)
    safe_expert = jnp.where(live_rows, expert, 0).astype(jnp.int32)
    within = (sorted_at - starts[safe_expert]).astype(jnp.int32)
    target = jnp.where(live_rows, safe_expert * capacity + within, 0).astype(jnp.int32)
    slot_ids = jnp.arange(capacity, dtype=jnp.int32)
    source = jnp.minimum(starts[:, None] + slot_ids[None, :], TOKENS - 1).reshape(-1).astype(jnp.int32)
    filled = (slot_ids[None, :] < expert_loads[:, None]).reshape(-1)
    picked = ordering[source]

    def forward(values, centroid_all, gains_all, shifts_all, first_all, bias_first, second_all, bias_second):
        sent_rows = low_back(values)
        live_weight = live_rows.astype(values.dtype)[:, None]
        fill_weight = filled.astype(values.dtype)[:, None]
        gathered = (sent_rows[picked] * fill_weight).reshape(expert_count, capacity, D)
        results = lax.map(jax.checkpoint(expert_rows), (gathered, centroid_all, gains_all, shifts_all, first_all, bias_first, second_all, bias_second))
        returned = results.reshape(expert_count * capacity, D)[target]
        return live_weight * (values + returned)
    float_args = [operand.astype(jnp.float32) for operand in (tokens, centroids, ln_gain, ln_bias, w_in, b_in, w_out, b_out)]
    result_out, pullback = jax.vjp(forward, *float_args)
    gradients = pullback(grad_output.astype(jnp.float32))
    return (result_out.astype(jnp.bfloat16), gradients[0].astype(jnp.bfloat16), gradients[1], gradients[2], gradients[3], gradients[4], gradients[5], gradients[6], gradients[7])
```

```python
import jax
import jax.numpy as jnp
from jax import lax
from jax.sharding import PartitionSpec as P

SEQ_LEN = 2048
EPSILON = 1e-05
F32 = jnp.float32
BF16 = jnp.bfloat16


def swap(value, mask):
    return lax.ppermute(value, "rep", [(r, r ^ mask) for r in range(lax.axis_size("rep"))])


def dot(left, right, contract):
    return lax.dot_general(left, right, (contract, ((), ())), preferred_element_type=F32)


def mm(left, right):
    return dot(left, right, ((1,), (0,)))


def mm_rt(left, right):
    return dot(left, right, ((1,), (1,)))


def mm_lt(left, right):
    return dot(left, right, ((0,), (0,)))


def ceil_to(value, unit):
    return -(-value // unit) * unit


def routing(lengths, assign, experts, slots):
    rows_here = assign.shape[0]
    device = lax.axis_index("ex") * lax.axis_size("rep") + lax.axis_index("rep")
    position = device * rows_here + jnp.arange(rows_here, dtype=jnp.int32)
    sequence = position // SEQ_LEN
    seq_match = sequence[:, None] == jnp.arange(lengths.shape[0], dtype=jnp.int32)[None, :]
    length_of = jnp.sum(jnp.where(seq_match, lengths[None, :], 0), 1)
    live = position % SEQ_LEN < length_of
    expert = assign[:, 0]
    hits = (expert[:, None] == jnp.arange(experts, dtype=jnp.int32)[None, :]) & live[:, None]
    row = jnp.arange(rows_here, dtype=jnp.int32)
    below = (row[None, :] < row[:, None]).astype(BF16)
    earlier = mm(below, hits.astype(BF16))
    slot = jnp.sum(jnp.where(hits, earlier, 0.0), 1).astype(jnp.int32)
    target = jnp.where(live, expert * slots + slot, -1)
    counts = jnp.sum(hits.astype(F32), 0)
    return live, target, counts


def normalize(hidden):
    center = hidden - jnp.mean(hidden, -1, keepdims=True)
    rstd = lax.rsqrt(jnp.mean(center * center, -1, keepdims=True) + EPSILON)
    return center * rstd, rstd


def gelu_both(a):
    c = 0.7978845608028654
    t = jnp.tanh(c * (a + 0.044715 * a * a * a))
    act = 0.5 * a * (1.0 + t)
    slope = 0.5 * (1.0 + t) + 0.5 * a * (1.0 - t * t) * (c * (1.0 + 3 * 0.044715 * a * a))
    return act.astype(BF16), slope.astype(BF16)


def sub_forward(hidden, gain, shift, first, bias, second):
    xhat, rstd = normalize(hidden)
    normed = (xhat * gain + shift).astype(BF16)
    acts, slopes, out = [], [], 0.0
    for q in range(2):
        act, slope = gelu_both(mm(normed, first[q]) + bias[q])
        acts.append(act)
        slopes.append(slope)
        out = out + mm(act, second[q])
    return normed, acts, slopes, out.astype(BF16)


def sub_backward(d_hidden, slopes, first, second):
    d_branch = d_hidden.astype(BF16)
    d_pre, d_low, out = [], [], 0.0
    for q in range(2):
        d_pre.append(mm_rt(d_branch, second[q]) * slopes[q].astype(F32))
        d_low.append(d_pre[q].astype(BF16))
        out = out + mm_rt(d_low[q], first[q])
    return d_branch, d_pre, d_low, out


def norm_backward(d_normed, hidden, gain):
    xhat, rstd = normalize(hidden)
    dx = d_normed * gain
    return (
        dx - jnp.mean(dx, -1, keepdims=True) - xhat * jnp.mean(dx * xhat, -1, keepdims=True)
    ) * rstd


def expert_group(cap, arrived, outgoing_g, target, live, tokens, grad_output, table, params):
    centroid, gain, shift, b_second, b_first, first, second = params
    experts, slots = lax.axis_size("ex"), target[1]
    target = target[0]
    g_arrived = lax.all_to_all(outgoing_g, "ex", split_axis=0, concat_axis=0, tiled=True)
    offset = earlier_sum(table)
    slot = jnp.arange(slots, dtype=jnp.int32)
    place = jnp.where(slot[None, :] < table[:, None], offset[:, None] + slot[None, :], -1).reshape(-1)
    pick = (jnp.arange(cap, dtype=jnp.int32)[:, None] == place[None, :]).astype(BF16)
    x_own = mm(pick, arrived).astype(BF16)
    x_far = swap(x_own, 2)
    rows = [x_own, x_far]
    gates = [jax.nn.sigmoid(mm(x, centroid.astype(BF16)[:, None])) for x in rows]

    part0, keep0 = [], []
    for x in rows:
        normed, acts, slopes, out = sub_forward(x.astype(F32), gain[0], shift[0], first[0], b_first[0], second[0])
        keep0.append((normed, acts, slopes))
        part0.append(out)
    back0 = [swap(part0[1], 2), swap(part0[0], 2)]
    g_own = mm(pick, g_arrived).astype(BF16)
    g_far = swap(g_own, 2)
    grads = [g_own, g_far]
    hidden1 = [
        x.astype(F32) + p.astype(F32) + b.astype(F32) + b_second[0]
        for x, p, b in zip(rows, part0, back0)
    ]
    part1, keep1 = [], []
    for h in hidden1:
        normed, acts, slopes, out = sub_forward(h, gain[1], shift[1], first[1], b_first[1], second[1])
        keep1.append((normed, acts, slopes))
        part1.append(out)
    back1 = swap(part1[1], 2)
    hidden2 = hidden1[0] + part1[0].astype(F32) + back1.astype(F32) + b_second[1]
    result = (gates[0] * hidden2).astype(BF16)
    spread = lambda value: mm_lt(pick, value).astype(BF16)
    returned = lax.all_to_all(spread(result), "ex", split_axis=0, concat_axis=0, tiled=True)

    incoming = [g.astype(F32) for g in grads]
    d_gate = jnp.sum(incoming[0] * hidden2, 1, keepdims=True)
    d_logit = (d_gate * gates[0] * (1.0 - gates[0])).astype(BF16).astype(F32)
    d_hidden2 = [gate * g for gate, g in zip(gates, incoming)]
    state1 = [sub_backward(d, k[2], first[1], second[1]) for d, k in zip(d_hidden2, keep1)]
    partial1 = [s[3].astype(BF16) for s in state1]
    recv1 = [swap(partial1[1], 2), swap(partial1[0], 2)]
    d_hidden1 = [
        d + norm_backward(p.astype(F32) + b.astype(F32), h, gain[1])
        for d, p, b, h in zip(d_hidden2, partial1, recv1, hidden1)
    ]
    state0 = [sub_backward(d, k[2], first[0], second[0]) for d, k in zip(d_hidden1, keep0)]
    partial0 = [s[3].astype(BF16) for s in state0]
    recv0 = swap(partial0[1], 2)
    d_hidden0 = d_hidden1[0] + norm_backward(
        partial0[0].astype(F32) + recv0.astype(F32), x_own.astype(F32), gain[0]
    )
    d_row = (d_hidden0 + d_logit * centroid).astype(BF16)
    d_back = lax.all_to_all(spread(d_row), "ex", split_axis=0, concat_axis=0, tiled=True)

    grads_first, grads_second, grads_bias = [], [], []
    for keep, state in ((keep0, state0), (keep1, state1)):
        w_first, w_second, bias = [], [], []
        for q in range(2):
            w_first.append(sum(mm_lt(k[0], s[2][q]) for k, s in zip(keep, state)))
            w_second.append(sum(mm_lt(k[1][q], s[0]) for k, s in zip(keep, state)))
            bias.append(sum(jnp.sum(s[1][q], 0) for s in state))
        grads_first.append(w_first[0] + swap(w_first[1].astype(BF16), 1).astype(F32))
        grads_second.append(w_second[0] + swap(w_second[1].astype(BF16), 1).astype(F32))
        grads_bias.append(bias)
    sib_bias = swap(jnp.stack([grads_bias[0][1], grads_bias[1][1]]), 1)
    grad_bias = jnp.stack([grads_bias[0][0], grads_bias[1][0]]) + sib_bias

    xhat0 = [normalize(x.astype(F32))[0] for x in rows]
    xhat1 = [normalize(h)[0] for h in hidden1]
    columns = jnp.stack([
        jnp.sum(d_logit * x_own.astype(F32), 0),
        sum(jnp.sum(s[3] * h, 0) for s, h in zip(state0, xhat0)),
        sum(jnp.sum(s[3] * h, 0) for s, h in zip(state1, xhat1)),
        sum(jnp.sum(s[3], 0) for s in state0),
        sum(jnp.sum(s[3], 0) for s in state1),
        jnp.sum(d_hidden1[0], 0),
        jnp.sum(d_hidden2[0], 0),
    ])
    columns = columns + swap(columns, 1)
    columns = columns + swap(columns, 2)
    width = columns.shape[1] // lax.axis_size("rep")
    columns = lax.dynamic_slice_in_dim(columns, lax.axis_index("rep") * width, width, 1)

    unpick = (target[:, None] == jnp.arange(experts * slots, dtype=jnp.int32)[None, :]).astype(BF16)
    alive = live[:, None]
    output = jnp.where(alive, tokens.astype(F32) + mm(unpick, returned), 0.0).astype(BF16)
    grad_input = jnp.where(alive, grad_output.astype(F32) + mm(unpick, d_back), 0.0).astype(BF16)
    return (
        output,
        grad_input,
        columns[0:1],
        columns[None, 1:3],
        columns[None, 3:5],
        jnp.stack(grads_first)[None],
        grad_bias[None],
        jnp.stack(grads_second)[None],
        columns[None, 5:7],
    )


def earlier_sum(counts):
    index = jnp.arange(counts.shape[0], dtype=jnp.int32)
    return jnp.sum(jnp.where(index[None, :] < index[:, None], counts[None, :], 0), 1)


def shards(
    tokens, lengths, assign, centroids, ln_gain, ln_bias, w_in, b_in, w_out, b_out, grad_output
):
    experts, reps = lax.axis_size("ex"), lax.axis_size("rep")
    rows_here = assign.shape[0]
    slots = ceil_to(max(2, 5 * rows_here // (4 * experts)), 8)
    live, target, counts = routing(lengths, assign, experts, slots)
    pack = (jnp.arange(experts * slots, dtype=jnp.int32)[:, None] == target[None, :]).astype(BF16)
    outgoing = mm(pack, tokens).astype(BF16)
    arrived = lax.all_to_all(outgoing, "ex", split_axis=0, concat_axis=0, tiled=True)
    outgoing_g = mm(pack, grad_output).astype(BF16)

    first_sib, second_sib, bias_sib = swap(w_in[0], 1), swap(w_out[0], 1), swap(b_in[0], 1)
    first = [[w_in[0, l], first_sib[l]] for l in range(2)]
    second = [[w_out[0, l], second_sib[l]] for l in range(2)]
    b_first = [[b_in[0, l].astype(F32)[None], bias_sib[l].astype(F32)[None]] for l in range(2)]

    width = centroids.shape[1]
    small = jnp.concatenate([centroids, ln_gain[0], ln_bias[0], b_out[0]], 0).reshape(-1)
    small = jnp.concatenate([counts.astype(BF16), small])
    everyone = lax.all_gather(small, ("ex", "rep"), axis=0, tiled=False).reshape(experts, reps, -1)
    e, r = lax.axis_index("ex"), lax.axis_index("rep")
    mine = lax.dynamic_index_in_dim(everyone[:, :, experts:], e, 0, keepdims=False)
    vectors = mine.reshape(reps, 7, width).transpose(1, 0, 2).reshape(7, 1, reps * width).astype(F32)
    counts_all = everyone[:, :, :experts].astype(F32)
    heaviest = jnp.max(jnp.sum(counts_all, 0))
    here = lax.dynamic_index_in_dim(counts_all, r, 1, keepdims=False)
    table = lax.dynamic_index_in_dim(here, e, 1, keepdims=False).astype(jnp.int32)

    params = (vectors[0, 0], vectors[1:3], vectors[3:5], vectors[5:7], b_first, first, second)
    worst = experts * slots
    caps = sorted({min(cap, worst) for cap in (576, 640)} | {worst})
    tier = sum((heaviest > cap).astype(jnp.int32) for cap in caps[:-1])

    operands = (arrived, outgoing_g, target, live, tokens, grad_output, table, params)

    def run(cap):
        def inner(arrived, outgoing_g, target, live, tokens, grad_output, table, params):
            return expert_group(
                cap, arrived, outgoing_g, (target, slots), live, tokens, grad_output, table, params
            )

        return inner

    return lax.switch(tier, [run(cap) for cap in caps], *operands)


def solution(mesh):
    rows = P(("ex", "rep"), None)
    in_specs = (
        rows,
        P(),
        rows,
        P("ex", "rep"),
        P("ex", None, "rep"),
        P("ex", None, "rep"),
        P("ex", None, None, "rep"),
        P("ex", None, "rep"),
        P("ex", None, "rep", None),
        P("ex", None, "rep"),
        rows,
    )
    out_specs = (
        rows,
        rows,
        P("ex", "rep"),
        P("ex", None, "rep"),
        P("ex", None, "rep"),
        P("ex", None, None, "rep"),
        P("ex", None, "rep"),
        P("ex", None, "rep", None),
        P("ex", None, "rep"),
    )
    return jax.shard_map(shards, mesh=mesh, in_specs=in_specs, out_specs=out_specs, check_vma=False)
```

```python
import functools

import jax
import jax.numpy as jnp
from jax import lax
from jax.experimental import pallas as pl
from jax.experimental.pallas import tpu as pltpu
from jax.sharding import PartitionSpec as P

SEQ_LEN = 2048
EPSILON = 1e-05
F32 = jnp.float32
BF16 = jnp.bfloat16
VMEM = pl.BlockSpec(memory_space=pltpu.VMEM)
SMEM = pl.BlockSpec(memory_space=pltpu.SMEM)
ANY = pl.BlockSpec(memory_space=pl.ANY)
HBM = pl.BlockSpec(memory_space=pltpu.HBM)
CAPS = (576, 640)
SCALE = 16


def swap(value, mask):
    return lax.ppermute(value, "rep", [(r, r ^ mask) for r in range(lax.axis_size("rep"))])


def dot(left, right, over_left, over_right):
    dims = (((over_left,), (over_right,)), ((), ()))
    return lax.dot_general(left, right, dims, preferred_element_type=F32)


def ceil_to(value, unit):
    return -(-value // unit) * unit


def shaped(*shape, dtype=BF16):
    return jax.ShapeDtypeStruct(shape, dtype)


def run(kernel, outs, operands, flops=0, scratch=(), in_specs=None, out_specs=None, limit=16, aliases=None, after=(), pinned=False, name=None):
    outs, count, extra = list(outs), len(operands), len(after)
    moved = sum(v.size * v.dtype.itemsize for v in (*operands, *outs))

    def body(*refs):
        kernel(*refs[:count], *refs[count + extra :])

    specs = in_specs or [VMEM] * count
    places = {id(HBM): pltpu.HBM, id(VMEM): pltpu.VMEM if pinned else pl.ANY}
    operands = [
        pltpu.with_memory_space_constraint(v, places.get(id(spec), pl.ANY))
        for v, spec in zip(operands, specs)
    ]
    out_specs = out_specs or [VMEM] * len(outs)
    outs = [
        pltpu.HBM(o.shape, o.dtype) if spec is HBM else o for o, spec in zip(outs, out_specs)
    ]
    return pl.pallas_call(
        body,
        out_shape=outs,
        in_specs=[*specs, *([ANY] * extra)],
        out_specs=out_specs,
        scratch_shapes=list(scratch),
        input_output_aliases=aliases or {},
        cost_estimate=pl.CostEstimate(flops=flops // SCALE, bytes_accessed=moved // SCALE, transcendentals=0),
        compiler_params=pltpu.CompilerParams(vmem_limit_bytes=limit << 20),
        name=name or kernel.__name__,
    )(*operands, *after)


def room(rows, limit):
    return dict(limit=limit, pinned=True) if rows <= 640 else dict(limit=54)


def iota(shape, dim):
    return lax.broadcasted_iota(jnp.int32, shape, dim)


def onehot(rows, index):
    return (iota((rows, index.shape[1]), 0) == index).astype(F32).astype(BF16)


def normalize(hidden):
    center = hidden - jnp.mean(hidden, -1, keepdims=True)
    rstd = lax.rsqrt(jnp.mean(center * center, -1, keepdims=True) + EPSILON)
    return center * rstd, rstd


def norm_backward(d_normed, xhat, rstd, gain):
    dx = d_normed * gain
    mean = jnp.mean(dx, -1, keepdims=True)
    return (dx - mean - xhat * jnp.mean(dx * xhat, -1, keepdims=True)) * rstd


def gelu_both(a):
    c = 0.7978845608028654
    a2 = a * a
    t = jnp.tanh(a * (c + (c * 0.044715) * a2))
    half = 0.5 + 0.5 * t
    act = a * half
    return act, half + act * (1.0 - t) * (c + (3 * c * 0.044715) * a2)


def gate_of(rows, centroid):
    return 1.0 / (1.0 + jnp.exp(-jnp.sum(rows * centroid, -1, keepdims=True)))


def up(ref):
    return ref[...].astype(F32)


CENTROID, GAIN, SHIFT, B_OUT = 0, 1, 3, 5


def row(ref, index):
    return ref[index : index + 1, :]


def route_kernel(experts, slots, lengths, base, assign, tokens, target_ref, count_ref, packed_ref):
    n = assign.shape[1]
    position = base[0] + iota((1, n), 1)
    first = base[0] // SEQ_LEN
    limit = jnp.zeros((1, n), jnp.int32)
    for k in range(n // SEQ_LEN + 2):
        s = first + k
        size = lengths[jnp.minimum(s, lengths.shape[0] - 1)]
        within = position - s * SEQ_LEN
        limit = jnp.where((within >= 0) & (within < size), 1, limit)
    live = limit > 0
    expert = assign[...]
    hits = ((iota((experts, n), 0) == expert) & live).astype(F32)
    before = (iota((n, n), 0) < iota((n, n), 1)).astype(F32).astype(BF16)
    earlier = dot(hits.astype(BF16), before, 1, 0)
    slot = jnp.sum(hits * earlier, 0, keepdims=True).astype(jnp.int32)
    target = jnp.where(live, expert * slots + slot, -1)
    target_ref[...] = target
    count_ref[...] = jnp.broadcast_to(jnp.sum(hits, 1, keepdims=True), count_ref.shape)
    packed_ref[...] = dot(onehot(experts * slots, target), tokens[...], 1, 0).astype(BF16)


def pack_kernel(target, values, counts, packed_ref, counts_ref):
    counts_ref[...] = counts[...]
    packed_ref[...] = dot(onehot(packed_ref.shape[0], target[...]), values[...], 1, 0).astype(BF16)


def unpack_kernel(target, returned, values, out_ref):
    places = onehot(returned.shape[0], target[...])
    moved = dot(places, returned[...], 0, 0)
    alive = dot(places, jnp.ones((returned.shape[0], 128), BF16), 0, 0)[:, 0:1] > 0.5
    out_ref[...] = jnp.where(alive, up(values) + moved, 0.0).astype(BF16)


def compact_kernel(place, arrived, rows_ref):
    rows_ref[...] = dot(onehot(rows_ref.shape[0], place[...]), arrived[...], 1, 0).astype(BF16)


def spread(place, values, slots_ref):
    places = onehot(values.shape[0], place[...])
    slots_ref[...] = dot(places, values, 0, 0).astype(BF16)


def hidden1_of(rows, own0, far0, vectors):
    return up(rows) + up(own0) + up(far0) + row(vectors, B_OUT)


def hold(value, after):
    return run(
        hold_kernel, [shaped(*value.shape)], [value], in_specs=[HBM], out_specs=[HBM], aliases={0: 0}, after=after
    )[0]


def hold_kernel(value, same):
    pass


class Copies:
    def __init__(self, sems):
        self.sems, self.made = sems, []

    def start(self, source, target):
        copy = pltpu.make_async_copy(source, target, self.sems.at[len(self.made)])
        copy.start()
        self.made.append(copy)
        return copy

    def wait(self):
        for copy in self.made:
            copy.wait()


def fetch(layer, weights, order, buffer, sems):
    copies = [
        pltpu.make_async_copy(weights[k].at[layer], buffer.at[k], sems.at[k]) for k in range(4)
    ]
    copies[order[0]].start()
    copies[order[1]].start()
    left = list(order)

    def got(k):
        assert left.pop(0) == k
        copies[k].wait()
        if len(left) > 1:
            copies[left[1]].start()
        return buffer[k]

    return got


def dma(count):
    return pltpu.SemaphoreType.DMA((count,))


def weight_scratch(weights):
    return [pltpu.VMEM((4, *weights[0].shape[1:]), BF16), dma(4)]


def forward_kernel(layer, *refs):
    n = 1 + 2 * layer
    sources, (vectors, biases_own, biases_sib) = refs[:n], refs[n : n + 3]
    got = fetch(layer, refs[n + 3 : n + 7], (0, 2, 1, 3), *refs[-2:])
    normed_out, act_out, slope_out, out_ref, normed, act, slope, sems = refs[n + 7 : n + 15]
    copies = Copies(sems)
    hidden = hidden1_of(*sources, vectors) if layer else up(sources[0])
    xhat, _ = normalize(hidden)
    normed[...] = (xhat * row(vectors, GAIN + layer) + row(vectors, SHIFT + layer)).astype(BF16)
    copies.start(normed, normed_out)
    total = None
    for q, bias in enumerate((biases_own, biases_sib)):
        pre = dot(normed[...], got(q), 1, 0) + row(bias, layer).astype(F32)
        columns = slice(q * pre.shape[1], (q + 1) * pre.shape[1])
        value, change = gelu_both(pre)
        act[:, columns] = value.astype(BF16)
        slope[:, columns] = change.astype(BF16)
        copies.start(act.at[:, columns], act_out.at[:, columns])
        copies.start(slope.at[:, columns], slope_out.at[:, columns])
        part = dot(act[:, columns], got(2 + q), 1, 0)
        total = part if total is None else total + part
    out_ref[...] = total.astype(BF16)
    copies.wait()


def forward(layer, sources, vectors, biases, weights, after=()):
    rows, d = sources[0].shape
    f = 2 * weights[0].shape[2]
    small = [*sources, vectors, *biases]
    return run(
        functools.partial(forward_kernel, layer),
        [shaped(rows, d), shaped(rows, f), shaped(rows, f), shaped(rows, d)],
        [*small, *weights],
        flops=4 * rows * d * f,
        in_specs=[VMEM] * len(small) + [HBM] * 4,
        out_specs=[HBM] * 3 + [VMEM],
        scratch=[
            pltpu.VMEM((rows, d), BF16),
            pltpu.VMEM((rows, f), BF16),
            pltpu.VMEM((rows, f), BF16),
            dma(5),
            *weight_scratch(weights),
        ],
        after=after,
        name=f"forward_sublayer{layer}",
        **room(rows, 26),
    )


def backward_kernel(layer, keep, *refs):
    n = 4 if layer else 6
    sources, (vectors, slope_in) = refs[:n], refs[n : n + 2]
    got = fetch(layer, refs[n + 2 : n + 6], (2, 0, 3, 1), *refs[-2:])
    branch_out, low_out, out_ref, columns_ref, bias_ref = refs[n + 6 : n + 11]
    branch, low, slope, sems, slope_sem = refs[-7:-2]
    copies = Copies(sems)
    slope_copy = pltpu.make_async_copy(slope_in, slope, slope_sem.at[0])
    slope_copy.start()
    rows, grads, own0, far0 = sources[:4]
    d_hidden = gate_of(up(rows), row(vectors, CENTROID)) * up(grads)
    if layer == 0:
        xhat, rstd = normalize(hidden1_of(rows, own0, far0, vectors))
        d_normed = up(sources[4]) + up(sources[5])
        d_hidden = d_hidden + norm_backward(d_normed, xhat, rstd, row(vectors, GAIN + 1))
        if keep:
            refs[n + 11][...] = d_hidden
    branch[...] = d_hidden.astype(BF16)
    copies.start(branch, branch_out)
    columns_ref[2:3, :] = jnp.sum(d_hidden, 0, keepdims=True)
    total = None
    for q in range(2):
        d_act = dot(branch[...], got(2 + q), 1, 1)
        if q == 0:
            slope_copy.wait()
        columns = slice(q * d_act.shape[1], (q + 1) * d_act.shape[1])
        d_pre = d_act * slope[:, columns].astype(F32)
        bias_ref[:, columns] = jnp.sum(d_pre, 0, keepdims=True)
        low[:, columns] = d_pre.astype(BF16)
        copies.start(low.at[:, columns], low_out.at[:, columns])
        part = dot(low[:, columns], got(q), 1, 1)
        total = part if total is None else total + part
    out_ref[...] = total.astype(BF16)
    xhat, _ = normalize(hidden1_of(rows, own0, far0, vectors) if layer else up(rows))
    columns_ref[0:1, :] = jnp.sum(total * xhat, 0, keepdims=True)
    columns_ref[1:2, :] = jnp.sum(total, 0, keepdims=True)
    copies.wait()


def backward(layer, keep, sources, vectors, slope, weights, after=()):
    rows, d = sources[0].shape
    f = 2 * weights[0].shape[2]
    outs = [shaped(rows, d), shaped(rows, f), shaped(rows, d), shaped(3, d, dtype=F32), shaped(1, f, dtype=F32)]
    outs += [shaped(rows, d, dtype=F32)] if keep else []
    return run(
        functools.partial(backward_kernel, layer, keep),
        outs,
        [*sources, vectors, slope, *weights],
        flops=4 * rows * d * f,
        in_specs=[VMEM] * (len(sources) + 1) + [HBM] * 5,
        out_specs=[HBM] * 2 + [VMEM] * (len(outs) - 2),
        scratch=[
            pltpu.VMEM((rows, d), BF16),
            pltpu.VMEM((rows, f), BF16),
            pltpu.VMEM((rows, f), BF16),
            dma(3),
            dma(1),
            *weight_scratch(weights),
        ],
        after=after,
        name=f"backward_sublayer{layer}",
        **room(rows, 26),
    )


def result_kernel(place, rows, grads, own0, far0, own1, far1, vectors, slots_ref, logit_ref):
    gate = gate_of(up(rows), row(vectors, CENTROID))
    hidden = hidden1_of(rows, own0, far0, vectors) + up(own1) + up(far1) + row(vectors, B_OUT + 1)
    d_gate = jnp.sum(up(grads) * hidden, -1, keepdims=True)
    d_logit = (d_gate * gate * (1.0 - gate)).astype(BF16).astype(F32)
    logit_ref[...] = jnp.broadcast_to(d_logit, logit_ref.shape)
    spread(place, (gate * hidden).astype(BF16), slots_ref)


def row_grad_kernel(place, rows, d_hidden1, logit, own0, far0, vectors, slots_ref, columns_ref):
    x = up(rows)
    xhat, rstd = normalize(x)
    d_logit = logit[:, 0:1]
    d_hidden = d_hidden1[...] + norm_backward(up(own0) + up(far0), xhat, rstd, row(vectors, GAIN))
    d_row = d_hidden + d_logit * row(vectors, CENTROID)
    spread(place, d_row.astype(BF16), slots_ref)
    columns_ref[...] = jnp.sum(d_logit * x, 0, keepdims=True)


def products(q, sources, buffers, sems):
    width = sources[2].shape[1] // 2
    columns = slice(q * width, (q + 1) * width)
    wide = (2, 3, 4, 5)
    order = (0, 2, 1, 3, 4, 6, 5, 7)
    copies = {
        k: pltpu.make_async_copy(
            sources[k].at[:, columns] if k in wide else sources[k], buffers[k], sems.at[k]
        )
        for k in order
    }
    for k in order:
        copies[k].start()

    def got(k):
        if k in copies:
            copies.pop(k).wait()
        return buffers[k]

    def first(part):
        return sum(dot(got(k)[...], got(2 + k)[:, part], 0, 0) for k in range(2))

    def second(part):
        return sum(dot(got(4 + k)[:, part], got(6 + k)[...], 0, 0) for k in range(2))

    return first, second, width


def sibling_kernel(*refs):
    first_ref, second_ref, bias_ref = refs[10:13]
    first, second, width = products(1, refs[:8], refs[13:21], refs[21])
    half = width // 2
    parts = [slice(k * half, (k + 1) * half) for k in range(2)]
    for part in parts:
        first_ref[:, part] = first(part).astype(BF16)
    for part in parts:
        second_ref[part, :] = second(part).astype(BF16)
    bias_ref[...] = (refs[8][...] + refs[9][...])[:, width:]


def own_kernel(layer, n_before, *refs):
    got_first_in, got_second_in, got_bias = refs[10:13]
    refs_out = refs[13 + n_before :]
    first_out, second_out, bias_ref = refs_out[:3]
    first, second, width = products(0, refs[:8], refs_out[3:11], refs_out[11])
    got_first, got_second, buffer_first, buffer_second, sems_in, sems = refs_out[12:]
    copies_in = Copies(sems_in)
    copy_first = copies_in.start(got_first_in, got_first)
    copy_second = copies_in.start(got_second_in, got_second)
    half = width // 2
    parts = [slice(k * half, (k + 1) * half) for k in range(2)]
    copies = Copies(sems)
    for k, part in enumerate(parts):
        value = first(part)
        if k == 0:
            copy_first.wait()
        buffer_first[:, part] = value + got_first[:, part].astype(F32)
        copies.start(buffer_first.at[:, part], first_out.at[layer, :, part])
    for k, part in enumerate(parts):
        value = second(part)
        if k == 0:
            copy_second.wait()
        buffer_second[part, :] = value + got_second[part, :].astype(F32)
        copies.start(buffer_second.at[part, :], second_out.at[layer, part, :])
    bias_ref[...] = (refs[8][...] + refs[9][...])[:, :width] + got_bias[...]
    copies.wait()


def product_scratch(saved):
    rows, d = saved[0][0].shape
    f = saved[1][0].shape[1] // 2
    return [pltpu.VMEM((rows, n), BF16) for n in (d, d, f, f, f, f, d, d)] + [dma(8)]


def sibling_grads(saved, biases, after=()):
    normed, low, act, branch = saved
    rows, d = normed[0].shape
    f = low[0].shape[1] // 2
    return run(
        sibling_kernel,
        [shaped(d, f), shaped(f, d), shaped(1, f, dtype=F32)],
        [*normed, *low, *act, *branch, *biases],
        flops=8 * rows * d * f,
        in_specs=[HBM] * 8 + [VMEM] * 2,
        scratch=product_scratch(saved),
        after=after,
        **room(rows, 24),
    )


def own_grads(layer, saved, biases, got, before, after=()):
    normed, low, act, branch = saved
    rows, d = normed[0].shape
    f = low[0].shape[1] // 2
    return run(
        functools.partial(own_kernel, layer, len(before)),
        [shaped(2, d, f, dtype=F32), shaped(2, f, d, dtype=F32), shaped(1, f, dtype=F32)],
        [*normed, *low, *act, *branch, *biases, *got, *before],
        flops=8 * rows * d * f,
        in_specs=[HBM] * 8 + [VMEM] * 2 + [HBM] * 2 + [VMEM] + [HBM] * len(before),
        out_specs=[HBM, HBM, VMEM],
        scratch=[
            *product_scratch(saved),
            pltpu.VMEM((d, f), BF16),
            pltpu.VMEM((f, d), BF16),
            pltpu.VMEM((d, f), F32),
            pltpu.VMEM((f, d), F32),
            dma(2),
            dma(4),
        ],
        aliases={13 + k: k for k in range(len(before))},
        after=after,
        name=f"own_grads_sublayer{layer}",
        **room(rows, 32),
    )


def expert_group(cap, arrived, outgoing_g, target, place, tokens, grad_output, vectors, biases, weights):
    d = tokens.shape[1]
    worst = arrived.shape[0]
    exchange = functools.partial(lax.all_to_all, axis_name="ex", split_axis=0, concat_axis=0, tiled=True)
    one_hot_flops = 2 * cap * worst * d

    def compact(values):
        return run(compact_kernel, [shaped(cap, d)], [place, values], flops=one_hot_flops)[0]

    def unpack(returned, values):
        return run(unpack_kernel, [shaped(*values.shape)], [target, returned, values], flops=one_hot_flops)[0]

    x_own = compact(arrived)
    x_far = swap(x_own, 2)

    normed_own0, act_own0, slope_own0, own0 = forward(0, (x_own,), vectors, biases, weights)
    got_far0 = swap(own0, 2)
    normed_far0, act_far0, slope_far0, far0 = forward(0, (x_far,), vectors, biases, weights, (own0,))
    got_own0 = swap(far0, 2)
    g_arrived = exchange(hold(outgoing_g, (x_own,)))
    g_own = compact(g_arrived)
    g_far = swap(g_own, 2)

    normed_far1, act_far1, slope_far1, far1 = forward(1, (x_far, far0, got_far0), vectors, biases, weights)
    got_own1 = swap(far1, 2)
    normed_own1, act_own1, slope_own1, own1 = forward(1, (x_own, own0, got_own0), vectors, biases, weights)
    in_own, in_far = (x_own, g_own, own0, got_own0), (x_far, g_far, far0, got_far0)
    branch_own1, low_own1, d_own1, columns_own1, bias_own1 = backward(
        1, False, in_own, vectors, slope_own1, weights
    )
    got_d_far1 = swap(d_own1, 2)
    branch_far1, low_far1, d_far1, columns_far1, bias_far1 = backward(
        1, False, in_far, vectors, slope_far1, weights
    )
    got_d_own1 = swap(d_far1, 2)

    result, logit = run(
        result_kernel,
        [shaped(worst, d), shaped(cap, 128, dtype=F32)],
        [place, x_own, g_own, own0, got_own0, own1, got_own1, vectors],
        flops=one_hot_flops,
    )
    returned = exchange(result)

    saved1 = (
        (normed_own1, normed_far1),
        (low_own1, low_far1),
        (act_own1, act_far1),
        (branch_own1, branch_far1),
    )
    sent1 = sibling_grads(saved1, (bias_own1, bias_far1))
    got1 = [swap(v, 1) for v in sent1]

    branch_far0, low_far0, d_far0, columns_far0, bias_far0 = backward(
        0, False, (*in_far, d_far1, got_d_far1), vectors, slope_far0, weights, (sent1[2],)
    )
    got_d_own0 = swap(d_far0, 2)
    grad_first, grad_second, grad_bias1 = own_grads(
        1, saved1, (bias_own1, bias_far1), got1, (), (bias_far0,)
    )
    branch_own0, low_own0, d_own0, columns_own0, bias_own0, d_hidden1 = backward(
        0, True, (*in_own, d_own1, got_d_own1), vectors, slope_own0, weights, (grad_bias1,)
    )
    d_rows, columns_x = run(
        row_grad_kernel,
        [shaped(worst, d), shaped(1, d, dtype=F32)],
        [place, x_own, d_hidden1, logit, d_own0, got_d_own0, vectors],
        flops=one_hot_flops,
    )
    d_back = exchange(d_rows)

    saved0 = (
        (normed_own0, normed_far0),
        (low_own0, low_far0),
        (act_own0, act_far0),
        (branch_own0, branch_far0),
    )
    sent0 = sibling_grads(saved0, (bias_own0, bias_far0), (columns_x,))
    got0 = [swap(v, 1) for v in sent0]
    grad_first, grad_second, grad_bias0 = own_grads(
        0, saved0, (bias_own0, bias_far0), got0, (grad_first, grad_second)
    )

    both0, both1 = columns_own0 + columns_far0, columns_own1 + columns_far1
    columns = jnp.concatenate(
        [columns_x, both0[0:1], both1[0:1], both0[1:2], both1[1:2], columns_own0[2:3], columns_own1[2:3]]
    )
    columns = columns + swap(columns, 1)
    columns = columns + swap(columns, 2)
    width = d // lax.axis_size("rep")
    columns = lax.dynamic_slice_in_dim(columns, lax.axis_index("rep") * width, width, 1)

    return (
        unpack(returned, tokens),
        unpack(d_back, grad_output),
        columns[0:1],
        columns[None, 1:3],
        columns[None, 3:5],
        grad_first[None],
        jnp.concatenate([grad_bias0, grad_bias1])[None],
        grad_second[None],
        columns[None, 5:7],
    )


def shards(
    tokens, lengths, assign, centroids, ln_gain, ln_bias, w_in, b_in, w_out, b_out, grad_output
):
    experts, reps = lax.axis_size("ex"), lax.axis_size("rep")
    rows_here, d = tokens.shape
    slots = ceil_to(max(2, 5 * rows_here // (4 * experts)), 8)
    worst = experts * slots
    e, r = lax.axis_index("ex"), lax.axis_index("rep")
    base = ((e * reps + r) * rows_here).astype(jnp.int32).reshape(1)
    target, counts, outgoing = run(
        functools.partial(route_kernel, experts, slots),
        [shaped(1, rows_here, dtype=jnp.int32), shaped(experts, 128, dtype=F32), shaped(worst, d)],
        [lengths, base, assign.reshape(1, rows_here), tokens],
        in_specs=[SMEM, SMEM, VMEM, VMEM],
        name="route",
        flops=2 * worst * rows_here * d,
    )
    arrived = lax.all_to_all(outgoing, "ex", split_axis=0, concat_axis=0, tiled=True)
    outgoing_g, counts = run(
        pack_kernel,
        [shaped(worst, d), shaped(experts, 128, dtype=F32)],
        [target, grad_output, counts],
        flops=2 * worst * rows_here * d,
    )

    biases = (b_in[0], swap(b_in[0], 1))
    weights = (w_in[0], swap(w_in[0], 1), w_out[0], swap(w_out[0], 1))

    width = centroids.shape[1]
    row_of_counts = jnp.pad(counts[:, 0].astype(BF16), (0, width - experts))[None]
    small = jnp.concatenate([centroids, ln_gain[0], ln_bias[0], b_out[0], row_of_counts], 0)
    gathered = lax.all_gather(small, "rep", axis=1, tiled=True)
    vectors = gathered.astype(F32)
    group = gathered[7].reshape(reps, width)
    counts_all = lax.all_gather(group[:, :experts], "ex", axis=0, tiled=False).astype(F32)
    heaviest = jnp.max(jnp.sum(counts_all, 0))
    here = lax.dynamic_index_in_dim(counts_all, r, 1, keepdims=False)
    table = lax.dynamic_index_in_dim(here, e, 1, keepdims=False).astype(jnp.int32)

    index, slot = jnp.arange(experts, dtype=jnp.int32), jnp.arange(slots, dtype=jnp.int32)
    offset = jnp.sum(jnp.where(index[None, :] < index[:, None], table[None, :], 0), 1)
    place = jnp.where(slot[None, :] < table[:, None], offset[:, None] + slot[None, :], -1)
    place = place.reshape(1, worst)

    caps = sorted({min(cap, worst) for cap in CAPS} | {worst})
    tier = sum((heaviest > cap).astype(jnp.int32) for cap in caps[:-1])
    return lax.switch(
        tier,
        [functools.partial(expert_group, cap) for cap in caps],
        *(arrived, outgoing_g, target, place, tokens, grad_output, vectors, biases, weights),
    )


def solution(mesh):
    rows = P(("ex", "rep"), None)
    in_specs = (
        rows,
        P(),
        rows,
        P("ex", "rep"),
        P("ex", None, "rep"),
        P("ex", None, "rep"),
        P("ex", None, None, "rep"),
        P("ex", None, "rep"),
        P("ex", None, "rep", None),
        P("ex", None, "rep"),
        rows,
    )
    out_specs = (
        rows,
        rows,
        P("ex", "rep"),
        P("ex", None, "rep"),
        P("ex", None, "rep"),
        P("ex", None, None, "rep"),
        P("ex", None, "rep"),
        P("ex", None, "rep", None),
        P("ex", None, "rep"),
    )
    return jax.shard_map(shards, mesh=mesh, in_specs=in_specs, out_specs=out_specs, check_vma=False)
```

```python
import functools

import jax
import jax.numpy as jnp
from jax import lax
from jax.experimental import pallas as pl
from jax.experimental.pallas import tpu as pltpu
from jax.sharding import PartitionSpec as P

SEQ_LEN = 2048
EPSILON = 1e-05
F32 = jnp.float32
BF16 = jnp.bfloat16
VMEM = pl.BlockSpec(memory_space=pltpu.VMEM)
SMEM = pl.BlockSpec(memory_space=pltpu.SMEM)
ANY = pl.BlockSpec(memory_space=pl.ANY)
HBM = pl.BlockSpec(memory_space=pltpu.HBM)
CAP = 640
SCALE = 16


def swap(value, mask):
    return lax.ppermute(value, "rep", [(r, r ^ mask) for r in range(lax.axis_size("rep"))])


def dot(left, right, over_left, over_right):
    dims = (((over_left,), (over_right,)), ((), ()))
    return lax.dot_general(left, right, dims, preferred_element_type=F32)


def ceil_to(value, unit):
    return -(-value // unit) * unit


def shaped(*shape, dtype=BF16):
    return jax.ShapeDtypeStruct(shape, dtype)


def run(kernel, outs, operands, flops=0, scratch=(), in_specs=None, out_specs=None, limit=16, aliases=None, after=(), pinned=False, name=None):
    outs, count, extra = list(outs), len(operands), len(after)
    moved = sum(v.size * v.dtype.itemsize for v in (*operands, *outs))

    def body(*refs):
        kernel(*refs[:count], *refs[count + extra :])

    specs = in_specs or [VMEM] * count
    places = {id(HBM): pltpu.HBM, id(VMEM): pltpu.VMEM if pinned else pl.ANY}
    operands = [
        pltpu.with_memory_space_constraint(v, places.get(id(spec), pl.ANY))
        for v, spec in zip(operands, specs)
    ]
    out_specs = out_specs or [VMEM] * len(outs)
    outs = [
        pltpu.HBM(o.shape, o.dtype) if spec is HBM else o for o, spec in zip(outs, out_specs)
    ]
    return pl.pallas_call(
        body,
        out_shape=outs,
        in_specs=[*specs, *([ANY] * extra)],
        out_specs=out_specs,
        scratch_shapes=list(scratch),
        input_output_aliases=aliases or {},
        cost_estimate=pl.CostEstimate(flops=flops // SCALE, bytes_accessed=moved // SCALE, transcendentals=0),
        compiler_params=pltpu.CompilerParams(vmem_limit_bytes=limit << 20),
        name=name or kernel.__name__,
    )(*operands, *after)


def room(rows, limit):
    return dict(limit=limit, pinned=True) if rows <= 640 else dict(limit=54)


def iota(shape, dim):
    return lax.broadcasted_iota(jnp.int32, shape, dim)


def onehot(rows, index):
    return (iota((rows, index.shape[1]), 0) == index).astype(F32).astype(BF16)


def normalize(hidden):
    center = hidden - jnp.mean(hidden, -1, keepdims=True)
    rstd = lax.rsqrt(jnp.mean(center * center, -1, keepdims=True) + EPSILON)
    return center * rstd, rstd


def norm_backward(d_normed, xhat, rstd, gain):
    dx = d_normed * gain
    mean = jnp.mean(dx, -1, keepdims=True)
    return (dx - mean - xhat * jnp.mean(dx * xhat, -1, keepdims=True)) * rstd


def gelu_both(a):
    c = 0.7978845608028654
    a2 = a * a
    t = jnp.tanh(a * (c + (c * 0.044715) * a2))
    half = 0.5 + 0.5 * t
    act = a * half
    return act, half + act * (1.0 - t) * (c + (3 * c * 0.044715) * a2)


def gate_of(rows, centroid):
    return 1.0 / (1.0 + jnp.exp(-jnp.sum(rows * centroid, -1, keepdims=True)))


def up(ref):
    return ref[...].astype(F32)


CENTROID, GAIN, SHIFT, B_OUT = 0, 1, 3, 5


def row(ref, index):
    return ref[index : index + 1, :]


def route_kernel(experts, slots, lengths, base, assign, tokens, target_ref, packed_ref):
    n = assign.shape[1]
    position = base[0] + iota((1, n), 1)
    first = base[0] // SEQ_LEN
    limit = jnp.zeros((1, n), jnp.int32)
    for k in range(n // SEQ_LEN + 2):
        s = first + k
        size = lengths[jnp.minimum(s, lengths.shape[0] - 1)]
        within = position - s * SEQ_LEN
        limit = jnp.where((within >= 0) & (within < size), 1, limit)
    live = limit > 0
    expert = assign[...]
    hits = ((iota((experts, n), 0) == expert) & live).astype(F32)
    before = (iota((n, n), 0) < iota((n, n), 1)).astype(F32).astype(BF16)
    earlier = dot(hits.astype(BF16), before, 1, 0)
    slot = jnp.sum(hits * earlier, 0, keepdims=True).astype(jnp.int32)
    target = jnp.where(live, expert * slots + slot, -1)
    target_ref[...] = target
    packed = dot(onehot(experts * slots, target), tokens[...], 1, 0)
    packed_ref[...] = packed.astype(BF16)
    counts = jnp.broadcast_to(jnp.sum(hits, 1, keepdims=True), (experts, 128)).astype(BF16)
    last = iota((experts * slots, experts), 0) == iota((experts * slots, experts), 1) * slots + slots - 1
    marks = dot(last.astype(F32).astype(BF16), counts, 1, 0)
    packed_ref[:, 0:128] = (packed[:, 0:128] + marks).astype(BF16)


def pack_kernel(target, values, packed_ref):
    packed_ref[...] = dot(onehot(packed_ref.shape[0], target[...]), values[...], 1, 0).astype(BF16)


def marks_kernel(sources, returned, mark_ref):
    slots = returned.shape[0] // sources
    total = jnp.zeros((1, 128), F32)
    for k in range(sources):
        total = total + returned[(k + 1) * slots - 1 : (k + 1) * slots, 0:128].astype(F32)
    mark_ref[...] = jnp.zeros(mark_ref.shape, F32)
    mark_ref[:, 0:128] = total


def columns_kernel(column_x, own0, far0, own1, far1, mark, columns_ref):
    columns_ref[0:1, :] = column_x[...]
    columns_ref[1:2, :] = own0[0:1, :] + far0[0:1, :]
    columns_ref[2:3, :] = own1[0:1, :] + far1[0:1, :]
    columns_ref[3:4, :] = own0[1:2, :] + far0[1:2, :]
    columns_ref[4:5, :] = own1[1:2, :] + far1[1:2, :]
    columns_ref[5:6, :] = own0[2:3, :]
    columns_ref[6:7, :] = own1[2:3, :]
    columns_ref[7:8, :] = mark[...]


def add_kernel(left, right, out_ref):
    out_ref[...] = left[...] + right[...]


def finish_kernel(position, left, right, bias0, bias1, centroid_ref, gain_ref, shift_ref, out_ref, bias_ref, mark_ref):
    width = centroid_ref.shape[1]
    total = left[...] + right[...]
    mine = total[:, 0:width]
    for k in range(1, total.shape[1] // width):
        mine = jnp.where(position[0] == k, total[:, k * width : (k + 1) * width], mine)
    centroid_ref[...] = mine[0:1]
    gain_ref[...] = mine[1:3]
    shift_ref[...] = mine[3:5]
    out_ref[...] = mine[5:7]
    mark_ref[...] = total[7:8, 0:128]
    bias_ref[0:1, :] = bias0[...]
    bias_ref[1:2, :] = bias1[...]


def unpack_kernel(target, returned, values, out_ref):
    places = onehot(returned.shape[0], target[...])
    moved = dot(places, returned[...], 0, 0)
    alive = dot(places, jnp.ones((returned.shape[0], 128), BF16), 0, 0)[:, 0:1] > 0.5
    out_ref[...] = jnp.where(alive, up(values) + moved, 0.0).astype(BF16)


def compact_kernel(place, arrived, rows_ref):
    rows_ref[...] = dot(onehot(rows_ref.shape[0], place[...]), arrived[...], 1, 0).astype(BF16)


def place_kernel(sources, arrived, rows_ref, place_ref, count_ref):
    n = arrived.shape[0]
    slots = n // sources
    lane = iota((1, n), 1).astype(F32)
    place, total = jnp.full((1, n), -1.0, F32), jnp.zeros((1, 1), F32)
    for k in range(sources):
        count = arrived[(k + 1) * slots - 1 : (k + 1) * slots, 0:128].astype(F32)[:, 0:1]
        slot = lane - k * slots
        place = jnp.where((slot >= 0.0) & (slot < count), total + slot, place)
        total = total + count
    place_ref[...] = place.astype(jnp.int32)
    count_ref[...] = jnp.broadcast_to(total, count_ref.shape)
    rows_ref[...] = dot(onehot(rows_ref.shape[0], place_ref[...]), arrived[...], 1, 0).astype(BF16)


def spread(place, values, slots_ref):
    places = onehot(values.shape[0], place[...])
    slots_ref[...] = dot(places, values, 0, 0).astype(BF16)


def hidden1_of(rows, own0, far0, vectors):
    return up(rows) + up(own0) + up(far0) + row(vectors, B_OUT)


class Copies:
    def __init__(self, sems):
        self.sems, self.made = sems, []

    def start(self, source, target):
        copy = pltpu.make_async_copy(source, target, self.sems.at[len(self.made)])
        copy.start()
        self.made.append(copy)
        return copy

    def wait(self):
        for copy in self.made:
            copy.wait()


def fetch(layer, weights, order, buffer, sems):
    copies = [
        pltpu.make_async_copy(weights[k].at[layer], buffer.at[k], sems.at[k]) for k in range(4)
    ]
    copies[order[0]].start()
    copies[order[1]].start()
    left = list(order)

    def got(k):
        assert left.pop(0) == k
        copies[k].wait()
        if len(left) > 1:
            copies[left[1]].start()
        return buffer[k]

    return got


def dma(count):
    return pltpu.SemaphoreType.DMA((count,))


def weight_scratch(weights):
    return [pltpu.VMEM((4, *weights[0].shape[1:]), BF16), dma(4)]


def forward_kernel(layer, *refs):
    n = 1 + 2 * layer
    sources, (vectors, biases_own, biases_sib) = refs[:n], refs[n : n + 3]
    got = fetch(layer, refs[n + 3 : n + 7], (0, 2, 1, 3), *refs[-2:])
    normed_out, act_out, slope_out, out_ref, normed, act, slope, sems = refs[n + 7 : n + 15]
    copies = Copies(sems)
    hidden = hidden1_of(*sources, vectors) if layer else up(sources[0])
    xhat, _ = normalize(hidden)
    normed[...] = (xhat * row(vectors, GAIN + layer) + row(vectors, SHIFT + layer)).astype(BF16)
    copies.start(normed, normed_out)
    total = None
    for q, bias in enumerate((biases_own, biases_sib)):
        pre = dot(normed[...], got(q), 1, 0) + row(bias, layer).astype(F32)
        columns = slice(q * pre.shape[1], (q + 1) * pre.shape[1])
        value, change = gelu_both(pre)
        act[:, columns] = value.astype(BF16)
        slope[:, columns] = change.astype(BF16)
        copies.start(act.at[:, columns], act_out.at[:, columns])
        copies.start(slope.at[:, columns], slope_out.at[:, columns])
        part = dot(act[:, columns], got(2 + q), 1, 0)
        total = part if total is None else total + part
    out_ref[...] = total.astype(BF16)
    copies.wait()


def forward(layer, sources, vectors, biases, weights, after=()):
    rows, d = sources[0].shape
    f = 2 * weights[0].shape[2]
    small = [*sources, vectors, *biases]
    return run(
        functools.partial(forward_kernel, layer),
        [shaped(rows, d), shaped(rows, f), shaped(rows, f), shaped(rows, d)],
        [*small, *weights],
        flops=4 * rows * d * f,
        in_specs=[VMEM] * len(small) + [HBM] * 4,
        out_specs=[HBM] * 3 + [VMEM],
        scratch=[
            pltpu.VMEM((rows, d), BF16),
            pltpu.VMEM((rows, f), BF16),
            pltpu.VMEM((rows, f), BF16),
            dma(5),
            *weight_scratch(weights),
        ],
        after=after,
        name=f"forward_sublayer{layer}",
        **room(rows, 26),
    )


def backward_kernel(layer, keep, *refs):
    n = 4 if layer else 6
    sources, (vectors, slope_in) = refs[:n], refs[n : n + 2]
    got = fetch(layer, refs[n + 2 : n + 6], (2, 0, 3, 1), *refs[-2:])
    branch_out, low_out, out_ref, columns_ref, bias_ref = refs[n + 6 : n + 11]
    branch, low, slope, sems, slope_sem = refs[-7:-2]
    copies = Copies(sems)
    slope_copy = pltpu.make_async_copy(slope_in, slope, slope_sem.at[0])
    slope_copy.start()
    rows, grads, own0, far0 = sources[:4]
    d_hidden = gate_of(up(rows), row(vectors, CENTROID)) * up(grads)
    if layer == 0:
        xhat, rstd = normalize(hidden1_of(rows, own0, far0, vectors))
        d_normed = up(sources[4]) + up(sources[5])
        d_hidden = d_hidden + norm_backward(d_normed, xhat, rstd, row(vectors, GAIN + 1))
        if keep:
            refs[n + 11][...] = d_hidden
    branch[...] = d_hidden.astype(BF16)
    copies.start(branch, branch_out)
    columns_ref[2:3, :] = jnp.sum(d_hidden, 0, keepdims=True)
    total = None
    for q in range(2):
        d_act = dot(branch[...], got(2 + q), 1, 1)
        if q == 0:
            slope_copy.wait()
        columns = slice(q * d_act.shape[1], (q + 1) * d_act.shape[1])
        d_pre = d_act * slope[:, columns].astype(F32)
        bias_ref[:, columns] = jnp.sum(d_pre, 0, keepdims=True)
        low[:, columns] = d_pre.astype(BF16)
        copies.start(low.at[:, columns], low_out.at[:, columns])
        part = dot(low[:, columns], got(q), 1, 1)
        total = part if total is None else total + part
    out_ref[...] = total.astype(BF16)
    xhat, _ = normalize(hidden1_of(rows, own0, far0, vectors) if layer else up(rows))
    columns_ref[0:1, :] = jnp.sum(total * xhat, 0, keepdims=True)
    columns_ref[1:2, :] = jnp.sum(total, 0, keepdims=True)
    copies.wait()


def backward(layer, keep, sources, vectors, slope, weights, after=()):
    rows, d = sources[0].shape
    f = 2 * weights[0].shape[2]
    outs = [shaped(rows, d), shaped(rows, f), shaped(rows, d), shaped(3, d, dtype=F32), shaped(1, f, dtype=F32)]
    outs += [shaped(rows, d, dtype=F32)] if keep else []
    return run(
        functools.partial(backward_kernel, layer, keep),
        outs,
        [*sources, vectors, slope, *weights],
        flops=4 * rows * d * f,
        in_specs=[VMEM] * (len(sources) + 1) + [HBM] * 5,
        out_specs=[HBM] * 2 + [VMEM] * (len(outs) - 2),
        scratch=[
            pltpu.VMEM((rows, d), BF16),
            pltpu.VMEM((rows, f), BF16),
            pltpu.VMEM((rows, f), BF16),
            dma(3),
            dma(1),
            *weight_scratch(weights),
        ],
        after=after,
        name=f"backward_sublayer{layer}",
        **room(rows, 26),
    )


def result_kernel(sources, place, count, rows, grads, own0, far0, own1, far1, vectors, slots_ref, logit_ref):
    gate = gate_of(up(rows), row(vectors, CENTROID))
    hidden = hidden1_of(rows, own0, far0, vectors) + up(own1) + up(far1) + row(vectors, B_OUT + 1)
    d_gate = jnp.sum(up(grads) * hidden, -1, keepdims=True)
    d_logit = (d_gate * gate * (1.0 - gate)).astype(BF16).astype(F32)
    logit_ref[...] = jnp.broadcast_to(d_logit, logit_ref.shape)
    spread(place, (gate * hidden).astype(BF16), slots_ref)
    over = jnp.where(count[...] > rows.shape[0], 1.0, 0.0).astype(BF16)
    slots = slots_ref.shape[0] // sources
    for k in range(sources):
        slots_ref[(k + 1) * slots - 1 : (k + 1) * slots, 0:128] = over


def row_grad_kernel(place, rows, d_hidden1, logit, own0, far0, vectors, slots_ref, columns_ref):
    x = up(rows)
    xhat, rstd = normalize(x)
    d_logit = logit[:, 0:1]
    d_hidden = d_hidden1[...] + norm_backward(up(own0) + up(far0), xhat, rstd, row(vectors, GAIN))
    d_row = d_hidden + d_logit * row(vectors, CENTROID)
    spread(place, d_row.astype(BF16), slots_ref)
    columns_ref[...] = jnp.sum(d_logit * x, 0, keepdims=True)


def products(q, sources, buffers, sems):
    width = sources[2].shape[1] // 2
    columns = slice(q * width, (q + 1) * width)
    wide = (2, 3, 4, 5)
    order = (0, 2, 1, 3, 4, 6, 5, 7)
    copies = {
        k: pltpu.make_async_copy(
            sources[k].at[:, columns] if k in wide else sources[k], buffers[k], sems.at[k]
        )
        for k in order
    }
    for k in order:
        copies[k].start()

    def got(k):
        if k in copies:
            copies.pop(k).wait()
        return buffers[k]

    def first(part):
        return sum(dot(got(k)[...], got(2 + k)[:, part], 0, 0) for k in range(2))

    def second(part):
        return sum(dot(got(4 + k)[:, part], got(6 + k)[...], 0, 0) for k in range(2))

    return first, second, width


def sibling_kernel(*refs):
    first_ref, second_ref, bias_ref = refs[10:13]
    first, second, width = products(1, refs[:8], refs[13:21], refs[21])
    half = width // 2
    parts = [slice(k * half, (k + 1) * half) for k in range(2)]
    for part in parts:
        first_ref[:, part] = first(part).astype(BF16)
    for part in parts:
        second_ref[part, :] = second(part).astype(BF16)
    bias_ref[...] = (refs[8][...] + refs[9][...])[:, width:]


def own_kernel(layer, n_before, *refs):
    got_first_in, got_second_in, got_bias = refs[10:13]
    refs_out = refs[13 + n_before :]
    first_out, second_out, bias_ref = refs_out[:3]
    first, second, width = products(0, refs[:8], refs_out[3:11], refs_out[11])
    got_first, got_second, buffer_first, buffer_second, sems_in, sems = refs_out[12:]
    copies_in = Copies(sems_in)
    copy_first = copies_in.start(got_first_in, got_first)
    copy_second = copies_in.start(got_second_in, got_second)
    half = width // 2
    parts = [slice(k * half, (k + 1) * half) for k in range(2)]
    copies = Copies(sems)
    for k, part in enumerate(parts):
        value = first(part)
        if k == 0:
            copy_first.wait()
        buffer_first[:, part] = value + got_first[:, part].astype(F32)
        copies.start(buffer_first.at[:, part], first_out.at[layer, :, part])
    for k, part in enumerate(parts):
        value = second(part)
        if k == 0:
            copy_second.wait()
        buffer_second[part, :] = value + got_second[part, :].astype(F32)
        copies.start(buffer_second.at[part, :], second_out.at[layer, part, :])
    bias_ref[...] = (refs[8][...] + refs[9][...])[:, :width] + got_bias[...]
    copies.wait()


def product_scratch(saved):
    rows, d = saved[0][0].shape
    f = saved[1][0].shape[1] // 2
    return [pltpu.VMEM((rows, n), BF16) for n in (d, d, f, f, f, f, d, d)] + [dma(8)]


def sibling_grads(saved, biases, after=()):
    normed, low, act, branch = saved
    rows, d = normed[0].shape
    f = low[0].shape[1] // 2
    return run(
        sibling_kernel,
        [shaped(d, f), shaped(f, d), shaped(1, f, dtype=F32)],
        [*normed, *low, *act, *branch, *biases],
        flops=8 * rows * d * f,
        in_specs=[HBM] * 8 + [VMEM] * 2,
        scratch=product_scratch(saved),
        after=after,
        **room(rows, 24),
    )


def own_grads(layer, saved, biases, got, before, after=()):
    normed, low, act, branch = saved
    rows, d = normed[0].shape
    f = low[0].shape[1] // 2
    return run(
        functools.partial(own_kernel, layer, len(before)),
        [shaped(2, d, f, dtype=F32), shaped(2, f, d, dtype=F32), shaped(1, f, dtype=F32)],
        [*normed, *low, *act, *branch, *biases, *got, *before],
        flops=8 * rows * d * f,
        in_specs=[HBM] * 8 + [VMEM] * 2 + [HBM] * 2 + [VMEM] + [HBM] * len(before),
        out_specs=[HBM, HBM, VMEM],
        scratch=[
            *product_scratch(saved),
            pltpu.VMEM((d, f), BF16),
            pltpu.VMEM((f, d), BF16),
            pltpu.VMEM((d, f), F32),
            pltpu.VMEM((f, d), F32),
            dma(2),
            dma(4),
        ],
        aliases={13 + k: k for k in range(len(before))},
        after=after,
        name=f"own_grads_sublayer{layer}",
        **room(rows, 32),
    )


def expert_group(cap, arrived, outgoing_g, target, tokens, grad_output, vectors, biases, weights):
    d, worst, sources = tokens.shape[1], arrived.shape[0], lax.axis_size("ex")
    exchange = functools.partial(lax.all_to_all, axis_name="ex", split_axis=0, concat_axis=0, tiled=True)
    one_hot_flops = 2 * cap * worst * d

    def compact(values):
        return run(compact_kernel, [shaped(cap, d)], [place, values], flops=one_hot_flops)[0]

    def unpack(returned, values):
        return run(unpack_kernel, [shaped(*values.shape)], [target, returned, values], flops=one_hot_flops)[0]

    x_own, place, count = run(
        functools.partial(place_kernel, sources),
        [shaped(cap, d), shaped(1, worst, dtype=jnp.int32), shaped(1, 128, dtype=F32)],
        [arrived],
        flops=one_hot_flops,
        name="place",
        after=(vectors,),
    )
    x_far = swap(x_own, 2)

    normed_own0, act_own0, slope_own0, own0 = forward(0, (x_own,), vectors, biases, weights)
    got_far0 = swap(own0, 2)
    normed_far0, act_far0, slope_far0, far0 = forward(0, (x_far,), vectors, biases, weights, (own0,))
    got_own0 = swap(far0, 2)
    g_arrived = exchange(outgoing_g)
    g_own = compact(g_arrived)
    g_far = swap(g_own, 2)

    normed_far1, act_far1, slope_far1, far1 = forward(1, (x_far, far0, got_far0), vectors, biases, weights)
    got_own1 = swap(far1, 2)
    normed_own1, act_own1, slope_own1, own1 = forward(1, (x_own, own0, got_own0), vectors, biases, weights)
    in_own, in_far = (x_own, g_own, own0, got_own0), (x_far, g_far, far0, got_far0)
    branch_own1, low_own1, d_own1, columns_own1, bias_own1 = backward(
        1, False, in_own, vectors, slope_own1, weights
    )
    got_d_far1 = swap(d_own1, 2)
    branch_far1, low_far1, d_far1, columns_far1, bias_far1 = backward(
        1, False, in_far, vectors, slope_far1, weights
    )
    got_d_own1 = swap(d_far1, 2)

    result, logit = run(
        functools.partial(result_kernel, sources),
        [shaped(worst, d), shaped(cap, 128, dtype=F32)],
        [place, count, x_own, g_own, own0, got_own0, own1, got_own1, vectors],
        flops=one_hot_flops,
        name="result",
    )
    returned = exchange(result)

    saved1 = (
        (normed_own1, normed_far1),
        (low_own1, low_far1),
        (act_own1, act_far1),
        (branch_own1, branch_far1),
    )
    sent1 = sibling_grads(saved1, (bias_own1, bias_far1))
    got1 = [swap(v, 1) for v in sent1]

    branch_far0, low_far0, d_far0, columns_far0, bias_far0 = backward(
        0, False, (*in_far, d_far1, got_d_far1), vectors, slope_far0, weights, (sent1[2],)
    )
    got_d_own0 = swap(d_far0, 2)
    grad_first, grad_second, grad_bias1 = own_grads(
        1, saved1, (bias_own1, bias_far1), got1, (), (bias_far0,)
    )
    branch_own0, low_own0, d_own0, columns_own0, bias_own0, d_hidden1 = backward(
        0, True, (*in_own, d_own1, got_d_own1), vectors, slope_own0, weights, (grad_bias1,)
    )
    d_rows, columns_x = run(
        row_grad_kernel,
        [shaped(worst, d), shaped(1, d, dtype=F32)],
        [place, x_own, d_hidden1, logit, d_own0, got_d_own0, vectors],
        flops=one_hot_flops,
    )
    d_back = exchange(d_rows)

    saved0 = (
        (normed_own0, normed_far0),
        (low_own0, low_far0),
        (act_own0, act_far0),
        (branch_own0, branch_far0),
    )
    sent0 = sibling_grads(saved0, (bias_own0, bias_far0), (columns_x,))
    got0 = [swap(v, 1) for v in sent0]
    grad_first, grad_second, grad_bias0 = own_grads(
        0, saved0, (bias_own0, bias_far0), got0, (grad_first, grad_second)
    )

    marks = run(functools.partial(marks_kernel, sources), [shaped(1, d, dtype=F32)], [returned], name="marks")[0]
    row_sums = [columns_x, columns_own0, columns_far0, columns_own1, columns_far1, marks]
    columns = run(columns_kernel, [shaped(8, d, dtype=F32)], row_sums)[0]
    columns = run(add_kernel, [shaped(8, d, dtype=F32)], [columns, swap(columns, 1)])[0]
    width = d // lax.axis_size("rep")
    position = lax.axis_index("rep").astype(jnp.int32).reshape(1)
    *small, grad_bias, over = run(
        finish_kernel,
        [shaped(n, width, dtype=F32) for n in (1, 2, 2, 2)]
        + [shaped(2, grad_bias0.shape[1], dtype=F32), shaped(1, 128, dtype=F32)],
        [position, columns, swap(columns, 2), grad_bias0, grad_bias1],
        in_specs=[SMEM] + [VMEM] * 4,
    )
    outs = (
        unpack(returned, tokens),
        unpack(d_back, grad_output),
        small[0],
        small[1][None],
        small[2][None],
        grad_first[None],
        grad_bias[None],
        grad_second[None],
        small[3][None],
    )
    return outs, over[0, 0]


def shards(
    tokens, lengths, assign, centroids, ln_gain, ln_bias, w_in, b_in, w_out, b_out, grad_output
):
    experts, reps = lax.axis_size("ex"), lax.axis_size("rep")
    rows_here, d = tokens.shape
    slots = ceil_to(max(2, 5 * rows_here // (4 * experts)) + 1, 8)
    worst = experts * slots
    base = ((lax.axis_index("ex") * reps + lax.axis_index("rep")) * rows_here).astype(jnp.int32).reshape(1)
    target, outgoing = run(
        functools.partial(route_kernel, experts, slots),
        [shaped(1, rows_here, dtype=jnp.int32), shaped(worst, d)],
        [lengths, base, assign.reshape(1, rows_here), tokens],
        in_specs=[SMEM, SMEM, VMEM, VMEM],
        name="route",
        flops=2 * worst * rows_here * d,
    )
    arrived = lax.all_to_all(outgoing, "ex", split_axis=0, concat_axis=0, tiled=True)
    outgoing_g = run(pack_kernel, [shaped(worst, d)], [target, grad_output], flops=2 * worst * rows_here * d)[0]
    biases = (b_in[0], swap(b_in[0], 1))
    weights = (w_in[0], swap(w_in[0], 1), w_out[0], swap(w_out[0], 1))
    own_vectors = jnp.concatenate([centroids, ln_gain[0], ln_bias[0], b_out[0]], 0)
    own_vectors = jnp.concatenate([own_vectors, outgoing_g[:1, : own_vectors.shape[1]]], 0)
    vectors = lax.all_gather(own_vectors, "rep", axis=1, tiled=True).astype(F32)

    operands = (arrived, outgoing_g, target, tokens, grad_output, vectors, biases, weights)
    cap = min(CAP, worst)
    outs, over = expert_group(cap, *operands)
    if cap == worst:
        return outs
    return lax.cond(over > 0.0, lambda *_: expert_group(worst, *operands)[0], lambda *kept: kept, *outs)


def solution(mesh):
    rows = P(("ex", "rep"), None)
    in_specs = (
        rows,
        P(),
        rows,
        P("ex", "rep"),
        P("ex", None, "rep"),
        P("ex", None, "rep"),
        P("ex", None, None, "rep"),
        P("ex", None, "rep"),
        P("ex", None, "rep", None),
        P("ex", None, "rep"),
        rows,
    )
    out_specs = (
        rows,
        rows,
        P("ex", "rep"),
        P("ex", None, "rep"),
        P("ex", None, "rep"),
        P("ex", None, None, "rep"),
        P("ex", None, "rep"),
        P("ex", None, "rep", None),
        P("ex", None, "rep"),
    )
    return jax.shard_map(shards, mesh=mesh, in_specs=in_specs, out_specs=out_specs, check_vma=False)
```

```python
import functools

import jax
import jax.numpy as jnp
from jax import lax
from jax.experimental import pallas as pl
from jax.experimental.pallas import tpu as pltpu
from jax.sharding import PartitionSpec as P

SEQ_LEN = 2048
EPSILON = 1e-05
F32 = jnp.float32
BF16 = jnp.bfloat16
VMEM = pl.BlockSpec(memory_space=pltpu.VMEM)
SMEM = pl.BlockSpec(memory_space=pltpu.SMEM)
ANY = pl.BlockSpec(memory_space=pl.ANY)
HBM = pl.BlockSpec(memory_space=pltpu.HBM)
EDGE, SHARED = 448, 192
SCALE = 16
LAST_COST = 128


def swap(value, mask):
    return lax.ppermute(value, "rep", [(r, r ^ mask) for r in range(lax.axis_size("rep"))])


def dot(left, right, over_left, over_right):
    dims = (((over_left,), (over_right,)), ((), ()))
    return lax.dot_general(left, right, dims, preferred_element_type=F32)


def ceil_to(value, unit):
    return -(-value // unit) * unit


def shaped(*shape, dtype=BF16):
    return jax.ShapeDtypeStruct(shape, dtype)


def run(kernel, outs, operands, flops=0, scratch=(), in_specs=None, out_specs=None, limit=24, aliases=None, after=(), pinned=False, name=None):
    outs, count, extra = list(outs), len(operands), len(after)
    moved = sum(v.size * v.dtype.itemsize for v in (*operands, *outs))

    def body(*refs):
        kernel(*refs[:count], *refs[count + extra :])

    specs = in_specs or [VMEM] * count
    places = {id(HBM): pltpu.HBM, id(VMEM): pltpu.VMEM if pinned else pl.ANY}
    operands = [
        pltpu.with_memory_space_constraint(v, places.get(id(spec), pl.ANY))
        for v, spec in zip(operands, specs)
    ]
    out_specs = out_specs or [VMEM] * len(outs)
    outs = [
        pltpu.HBM(o.shape, o.dtype) if spec is HBM else o for o, spec in zip(outs, out_specs)
    ]
    return pl.pallas_call(
        body,
        out_shape=outs,
        in_specs=[*specs, *([ANY] * extra)],
        out_specs=out_specs,
        scratch_shapes=list(scratch),
        input_output_aliases=aliases or {},
        cost_estimate=pl.CostEstimate(flops=flops // SCALE, bytes_accessed=moved // SCALE, transcendentals=0),
        compiler_params=pltpu.CompilerParams(vmem_limit_bytes=limit << 20),
        name=name or kernel.__name__,
    )(*operands, *after)


def room(rows, limit):
    return dict(limit=limit, pinned=True) if rows <= 640 else dict(limit=54)


def iota(shape, dim):
    return lax.broadcasted_iota(jnp.int32, shape, dim)


def onehot(rows, index):
    return (iota((rows, index.shape[1]), 0) == index).astype(F32).astype(BF16)


def normalize(hidden):
    center = hidden - jnp.mean(hidden, -1, keepdims=True)
    rstd = lax.rsqrt(jnp.mean(center * center, -1, keepdims=True) + EPSILON)
    return center * rstd, rstd


def norm_backward(d_normed, xhat, rstd, gain):
    dx = d_normed * gain
    mean = jnp.mean(dx, -1, keepdims=True)
    return (dx - mean - xhat * jnp.mean(dx * xhat, -1, keepdims=True)) * rstd


def gelu_both(a):
    c = 0.7978845608028654
    a2 = a * a
    t = jnp.tanh(a * (c + (c * 0.044715) * a2))
    half = 0.5 + 0.5 * t
    act = a * half
    return act, half + act * (1.0 - t) * (c + (3 * c * 0.044715) * a2)


def gate_of(rows, centroid):
    return 1.0 / (1.0 + jnp.exp(-jnp.sum(rows * centroid, -1, keepdims=True)))


def up(ref):
    return ref[...].astype(F32)


CENTROID, GAIN, SHIFT, B_OUT = 0, 1, 3, 5


def row(ref, index):
    return ref[index : index + 1, :]


def route_kernel(experts, slots, lengths, base, assign, tokens, target_ref, packed_ref):
    n = assign.shape[1]
    position = base[0] + iota((1, n), 1)
    first = base[0] // SEQ_LEN
    limit = jnp.zeros((1, n), jnp.int32)
    for k in range(n // SEQ_LEN + 2):
        s = first + k
        size = lengths[jnp.minimum(s, lengths.shape[0] - 1)]
        within = position - s * SEQ_LEN
        limit = jnp.where((within >= 0) & (within < size), 1, limit)
    live = limit > 0
    expert = assign[...]
    hits = ((iota((experts, n), 0) == expert) & live).astype(F32)
    before = (iota((n, n), 0) < iota((n, n), 1)).astype(F32).astype(BF16)
    earlier = dot(hits.astype(BF16), before, 1, 0)
    slot = jnp.sum(hits * earlier, 0, keepdims=True).astype(jnp.int32)
    target = jnp.where(live, expert * slots + slot, -1)
    target_ref[...] = target
    packed = dot(onehot(experts * slots, target), tokens[...], 1, 0)
    packed_ref[...] = packed.astype(BF16)
    counts = jnp.broadcast_to(jnp.sum(hits, 1, keepdims=True), (experts, 128)).astype(BF16)
    last = iota((experts * slots, experts), 0) == iota((experts * slots, experts), 1) * slots + slots - 1
    marks = dot(last.astype(F32).astype(BF16), counts, 1, 0)
    packed_ref[:, 0:128] = (packed[:, 0:128] + marks).astype(BF16)


def pack_kernel(target, values, packed_ref):
    packed_ref[...] = dot(onehot(packed_ref.shape[0], target[...]), values[...], 1, 0).astype(BF16)


def marks_kernel(sources, returned, mark_ref):
    slots = returned.shape[0] // sources
    total = jnp.zeros((1, 128), F32)
    for k in range(sources):
        total = total + returned[(k + 1) * slots - 1 : (k + 1) * slots, 0:128].astype(F32)
    mark_ref[...] = jnp.zeros(mark_ref.shape, F32)
    mark_ref[:, 0:128] = total


def columns_kernel(column_x, own0, far0, own1, far1, mark, columns_ref):
    columns_ref[0:1, :] = column_x[...]
    columns_ref[1:2, :] = own0[0:1, :] + far0[0:1, :]
    columns_ref[2:3, :] = own1[0:1, :] + far1[0:1, :]
    columns_ref[3:4, :] = own0[1:2, :] + far0[1:2, :]
    columns_ref[4:5, :] = own1[1:2, :] + far1[1:2, :]
    columns_ref[5:6, :] = own0[2:3, :] + far0[2:3, :]
    columns_ref[6:7, :] = own1[2:3, :] + far1[2:3, :]
    columns_ref[7:8, :] = mark[...]


def add_kernel(left, right, out_ref):
    out_ref[...] = left[...] + right[...]


def finish_kernel(position, left, right, bias0, bias1, centroid_ref, gain_ref, shift_ref, out_ref, bias_ref, mark_ref):
    width = centroid_ref.shape[1]
    total = left[...] + right[...]
    mine = total[:, 0:width]
    for k in range(1, total.shape[1] // width):
        mine = jnp.where(position[0] == k, total[:, k * width : (k + 1) * width], mine)
    centroid_ref[...] = mine[0:1]
    gain_ref[...] = mine[1:3]
    shift_ref[...] = mine[3:5]
    out_ref[...] = mine[5:7]
    mark_ref[...] = total[7:8, 0:128]
    bias_ref[0:1, :] = bias0[...]
    bias_ref[1:2, :] = bias1[...]


def unpack_kernel(target, returned, values, out_ref):
    places = onehot(returned.shape[0], target[...])
    moved = dot(places, returned[...], 0, 0)
    alive = dot(places, jnp.ones((returned.shape[0], 128), BF16), 0, 0)[:, 0:1] > 0.5
    out_ref[...] = jnp.where(alive, up(values) + moved, 0.0).astype(BF16)


def compact_kernel(place, arrived, rows_ref):
    rows_ref[...] = dot(onehot(rows_ref.shape[0], place[...]), arrived[...], 1, 0).astype(BF16)


def place_kernel(senders, edge, position, arrived, rows_ref, place_ref, count_ref):
    n, window = arrived.shape[0], rows_ref.shape[0]
    slots = n // senders
    lane = iota((1, n), 1).astype(F32)
    place, total = jnp.full((1, n), -1.0, F32), jnp.zeros((1, 1), F32)
    for k in range(senders):
        count = arrived[(k + 1) * slots - 1 : (k + 1) * slots, 0:128].astype(F32)[:, 0:1]
        slot = lane - k * slots
        place = jnp.where((slot >= 0.0) & (slot < count), total + slot, place)
        total = total + count
    backwards = (place >= edge) & ((position[0] // 2) % 2 == 1)
    place = jnp.where(backwards, window + edge - 1 - place, place)
    place_ref[...] = place.astype(jnp.int32)
    count_ref[...] = jnp.broadcast_to(total, count_ref.shape)
    rows_ref[...] = dot(onehot(window, place_ref[...]), arrived[...], 1, 0).astype(BF16)


def spread(place, values, slots_ref):
    places = onehot(values.shape[0], place[...])
    slots_ref[...] = dot(places, values, 0, 0).astype(BF16)


FIELDS = {
    "p": ("pE", "pFW", "pFW"),
    "q": ("qOW", "qF", "qOW"),
    "d": ("dOW", "dF", "dOW"),
    "h": ("hE", "hFW", "hFW"),
    "c": ("cE", "cFW", "cFW"),
}


def names_of(rows, *fields):
    names = []
    for field in fields:
        if field in FIELDS:
            own, far, shared = FIELDS[field]
        else:
            own, far, shared = field + "_own", field + "_far", None
        names.append(own if rows in ("E", "OW") else far)
        if rows in ("OW", "FW"):
            names += [shared] if shared else [own, far]
    return list(dict.fromkeys(names))


def values_of(rows, field, edge, refs):
    if field in FIELDS:
        own, far, shared = FIELDS[field]
    else:
        own, far, shared = field + "_own", field + "_far", None
    first = refs[own if rows in ("E", "OW") else far]
    if rows in ("E", "F"):
        return first[0:edge, :].astype(F32)
    if shared:
        inner = refs[shared][edge:, :].astype(F32)
    else:
        inner = refs[own][edge:, :].astype(F32) + refs[far][edge:, :].astype(F32)
    return jnp.concatenate([first[0:edge, :].astype(F32), inner], 0)


def hidden1_of(rows, edge, refs, vectors):
    parts = [values_of(rows, field, edge, refs) for field in ("x", "p", "q")]
    return parts[0] + parts[1] + parts[2] + row(vectors, B_OUT)


class Copies:
    def __init__(self, sems):
        self.sems, self.made = sems, []

    def start(self, source, target):
        copy = pltpu.make_async_copy(source, target, self.sems.at[len(self.made)])
        copy.start()
        self.made.append(copy)
        return copy

    def wait(self):
        for copy in self.made:
            copy.wait()


def fetch(layer, weights, order, buffer, sems):
    copies = [
        pltpu.make_async_copy(weights[k].at[layer], buffer.at[k], sems.at[k]) for k in range(4)
    ]
    copies[order[0]].start()
    copies[order[1]].start()
    left = list(order)

    def got(k):
        assert left.pop(0) == k
        copies[k].wait()
        if len(left) > 1:
            copies[left[1]].start()
        return buffer[k]

    return got


def dma(count):
    return pltpu.SemaphoreType.DMA((count,))


def weight_scratch(weights):
    return [pltpu.VMEM((4, *weights[0].shape[1:]), BF16), dma(4)]


def forward_kernel(layer, rows, edge, names, send, *refs):
    n = len(names)
    named, (vectors, biases_own, biases_sib) = dict(zip(names, refs[:n])), refs[n : n + 3]
    got = fetch(layer, refs[n + 3 : n + 7], (0, 2, 1, 3), *refs[-2:])
    normed_out, act_out, slope_out, out_ref = refs[n + 7 : n + 11]
    normed, act, slope, sems = refs[-6:-2]
    copies = Copies(sems)
    hidden = hidden1_of(rows, edge, named, vectors) if layer else values_of(rows, "x", edge, named)
    xhat, _ = normalize(hidden)
    normed[...] = (xhat * row(vectors, GAIN + layer) + row(vectors, SHIFT + layer)).astype(BF16)
    copies.start(normed, normed_out)
    total = None
    for q, bias in enumerate((biases_own, biases_sib)):
        pre = dot(normed[...], got(q), 1, 0) + row(bias, layer).astype(F32)
        columns = slice(q * pre.shape[1], (q + 1) * pre.shape[1])
        value, change = gelu_both(pre)
        act[:, columns] = value.astype(BF16)
        slope[:, columns] = change.astype(BF16)
        copies.start(act.at[:, columns], act_out.at[:, columns])
        copies.start(slope.at[:, columns], slope_out.at[:, columns])
        part = dot(act[:, columns], got(2 + q), 1, 0)
        total = part if total is None else total + part
    out_ref[...] = total.astype(BF16)
    if send:
        refs[n + 11][...] = out_ref[edge:, :]
    copies.wait()


def forward(layer, rows, sizes, named, vectors, biases, weights, after=(), send=False):
    edge, count = sizes[0], sizes[0] + (sizes[1] if rows in ("OW", "FW") else 0)
    names = names_of(rows, *(("x", "p", "q") if layer else ("x",)))
    d, f = vectors.shape[1], 2 * weights[0].shape[2]
    small = [*(named[k] for k in names), vectors, *biases]
    return run(
        functools.partial(forward_kernel, layer, rows, edge, names, send),
        [shaped(count, d), shaped(count, f), shaped(count, f), shaped(count, d)] + [shaped(sizes[1], d)] * send,
        [*small, *weights],
        flops=4 * count * d * f,
        in_specs=[VMEM] * len(small) + [HBM] * 4,
        out_specs=[HBM] * 3 + [VMEM] * (1 + send),
        scratch=[
            pltpu.VMEM((count, d), BF16),
            pltpu.VMEM((count, f), BF16),
            pltpu.VMEM((count, f), BF16),
            dma(5),
            *weight_scratch(weights),
        ],
        after=after,
        name=f"forward_sublayer{layer}_{rows}",
        **room(count, 26),
    )


def backward_kernel(layer, rows, edge, names, *refs):
    n = len(names)
    named, (vectors, slope_in) = dict(zip(names, refs[:n])), refs[n : n + 2]
    got = fetch(layer, refs[n + 2 : n + 6], (2, 0, 3, 1), *refs[-2:])
    branch_out, low_out, out_ref, columns_ref, bias_ref = refs[n + 6 : n + 11]
    branch, low, slope, sems, slope_sem = refs[-7:-2]
    copies = Copies(sems)
    slope_copy = pltpu.make_async_copy(slope_in, slope, slope_sem.at[0])
    slope_copy.start()
    x = values_of(rows, "x", edge, named)
    d_hidden = gate_of(x, row(vectors, CENTROID)) * values_of(rows, "g", edge, named)
    if layer == 0:
        xhat, rstd = normalize(hidden1_of(rows, edge, named, vectors))
        d_normed = values_of(rows, "d", edge, named) + values_of(rows, "h", edge, named)
        d_hidden = d_hidden + norm_backward(d_normed, xhat, rstd, row(vectors, GAIN + 1))
        refs[n + 11][...] = d_hidden if rows == "E" else d_hidden[edge:]
    branch[...] = d_hidden.astype(BF16)
    copies.start(branch, branch_out)
    own = jnp.zeros((1, d_hidden.shape[1]), F32)
    if rows in ("E", "OW"):
        own = own + jnp.sum(d_hidden[:edge], 0, keepdims=True)
    if rows in ("OW", "FW"):
        own = own + 0.5 * jnp.sum(d_hidden[edge:], 0, keepdims=True)
    columns_ref[2:3, :] = own
    total = None
    for q in range(2):
        d_act = dot(branch[...], got(2 + q), 1, 1)
        if q == 0:
            slope_copy.wait()
        columns = slice(q * d_act.shape[1], (q + 1) * d_act.shape[1])
        d_pre = d_act * slope[:, columns].astype(F32)
        bias_ref[:, columns] = jnp.sum(d_pre, 0, keepdims=True)
        low[:, columns] = d_pre.astype(BF16)
        copies.start(low.at[:, columns], low_out.at[:, columns])
        part = dot(low[:, columns], got(q), 1, 1)
        total = part if total is None else total + part
    out_ref[...] = total.astype(BF16)
    xhat, _ = normalize(hidden1_of(rows, edge, named, vectors) if layer else values_of(rows, "x", edge, named))
    columns_ref[0:1, :] = jnp.sum(total * xhat, 0, keepdims=True)
    columns_ref[1:2, :] = jnp.sum(total, 0, keepdims=True)
    copies.wait()


def backward(layer, rows, sizes, named, vectors, slope, weights, after=()):
    edge, count = sizes[0], sizes[0] + (sizes[1] if rows in ("OW", "FW") else 0)
    names = names_of(rows, *(("x", "g", "p", "q") if layer else ("x", "g", "p", "q", "d", "h")))
    d, f = vectors.shape[1], 2 * weights[0].shape[2]
    outs = [shaped(count, d), shaped(count, f), shaped(count, d), shaped(3, d, dtype=F32), shaped(1, f, dtype=F32)]
    if layer == 0:
        outs.append(shaped(edge if rows == "E" else sizes[1], d, dtype=F32))
    operands = [named[k] for k in names]
    return run(
        functools.partial(backward_kernel, layer, rows, edge, names),
        outs,
        [*operands, vectors, slope, *weights],
        flops=(LAST_COST if layer == 0 and rows == "E" else 4) * count * d * f,
        in_specs=[VMEM] * (len(operands) + 1) + [HBM] * 5,
        out_specs=[HBM] * 2 + [VMEM] * (len(outs) - 2),
        scratch=[
            pltpu.VMEM((count, d), BF16),
            pltpu.VMEM((count, f), BF16),
            pltpu.VMEM((count, f), BF16),
            dma(3),
            dma(1),
            *weight_scratch(weights),
        ],
        after=after,
        name=f"backward_sublayer{layer}_{rows}",
        **room(count, 32),
    )


def result_kernel(senders, edge, names, *refs):
    named = dict(zip(names, refs))
    place, count, count_far, vectors, slots_ref, logit_ref = refs[len(names) :]
    gate = gate_of(values_of("OW", "x", edge, named), row(vectors, CENTROID))
    hidden = hidden1_of("OW", edge, named, vectors)
    hidden = hidden + up(named["u"]) + jnp.concatenate([up(named["vE"]), up(named["vS"])], 0) + row(vectors, B_OUT + 1)
    d_gate = jnp.sum(up(named["g_own"]) * hidden, -1, keepdims=True)
    d_logit = (d_gate * gate * (1.0 - gate)).astype(BF16).astype(F32)
    logit_ref[...] = jnp.broadcast_to(d_logit, logit_ref.shape)
    spread(place, (gate * hidden).astype(BF16), slots_ref)
    window = logit_ref.shape[0]
    inner = jnp.maximum(count[...] - edge, 0.0) + jnp.maximum(count_far[...] - edge, 0.0)
    over = jnp.where((count[...] > window) | (inner > window - edge), 1.0, 0.0).astype(BF16)
    slots = slots_ref.shape[0] // senders
    for k in range(senders):
        slots_ref[(k + 1) * slots - 1 : (k + 1) * slots, 0:128] = over


def row_grad_kernel(edge, names, *refs):
    named = dict(zip(names, refs))
    place, edge_grad, shared_grad, got, logit, vectors, slots_ref, columns_ref = refs[len(names) :]
    x = values_of("OW", "x", edge, named)
    xhat, rstd = normalize(x)
    d_logit = logit[:, 0:1]
    d_normed = values_of("OW", "c", edge, named) + up(got)
    d_hidden = jnp.concatenate([edge_grad[...], shared_grad[...]], 0)
    d_hidden = d_hidden + norm_backward(d_normed, xhat, rstd, row(vectors, GAIN))
    d_row = d_hidden + d_logit * row(vectors, CENTROID)
    spread(place, d_row.astype(BF16), slots_ref)
    columns_ref[...] = jnp.sum(d_logit * x, 0, keepdims=True)


def products(q, sources, buffers, sems):
    width = sources[2].shape[1] // 2
    columns = slice(q * width, (q + 1) * width)
    wide = (2, 3, 4, 5)
    order = (0, 2, 1, 3, 4, 6, 5, 7)
    copies = {
        k: pltpu.make_async_copy(
            sources[k].at[:, columns] if k in wide else sources[k], buffers[k], sems.at[k]
        )
        for k in order
    }
    for k in order:
        copies[k].start()

    def got(k):
        if k in copies:
            copies.pop(k).wait()
        return buffers[k]

    def first(part):
        return sum(dot(got(k)[...], got(2 + k)[:, part], 0, 0) for k in range(2))

    def second(part):
        return sum(dot(got(4 + k)[:, part], got(6 + k)[...], 0, 0) for k in range(2))

    return first, second, width


def sibling_kernel(*refs):
    first_ref, second_ref, bias_ref = refs[10:13]
    first, second, width = products(1, refs[:8], refs[13:21], refs[21])
    half = width // 2
    parts = [slice(k * half, (k + 1) * half) for k in range(2)]
    for part in parts:
        first_ref[:, part] = first(part).astype(BF16)
    for part in parts:
        second_ref[part, :] = second(part).astype(BF16)
    bias_ref[...] = (refs[8][...] + refs[9][...])[:, width:]


def own_kernel(layer, n_before, *refs):
    got_first_in, got_second_in, got_bias = refs[10:13]
    refs_out = refs[13 + n_before :]
    first_out, second_out, bias_ref = refs_out[:3]
    first, second, width = products(0, refs[:8], refs_out[3:11], refs_out[11])
    got_first, got_second, buffer_first, buffer_second, sems_in, sems = refs_out[12:]
    copies_in = Copies(sems_in)
    copy_first = copies_in.start(got_first_in, got_first)
    copy_second = copies_in.start(got_second_in, got_second)
    half = width // 2
    parts = [slice(k * half, (k + 1) * half) for k in range(2)]
    copies = Copies(sems)
    for k, part in enumerate(parts):
        value = first(part)
        if k == 0:
            copy_first.wait()
        buffer_first[:, part] = value + got_first[:, part].astype(F32)
        copies.start(buffer_first.at[:, part], first_out.at[layer, :, part])
    for k, part in enumerate(parts):
        value = second(part)
        if k == 0:
            copy_second.wait()
        buffer_second[part, :] = value + got_second[part, :].astype(F32)
        copies.start(buffer_second.at[part, :], second_out.at[layer, part, :])
    bias_ref[...] = (refs[8][...] + refs[9][...])[:, :width] + got_bias[...]
    copies.wait()


def product_scratch(saved):
    d, f = saved[0][0].shape[1], saved[1][0].shape[1] // 2
    counts = [v.shape[0] for v in saved[0]] * 4
    return [pltpu.VMEM((m, n), BF16) for m, n in zip(counts, (d, d, f, f, f, f, d, d))] + [dma(8)]


def sibling_grads(saved, biases, after=()):
    normed, low, act, branch = saved
    rows, d = sum(v.shape[0] for v in normed), normed[0].shape[1]
    f = low[0].shape[1] // 2
    return run(
        sibling_kernel,
        [shaped(d, f), shaped(f, d), shaped(1, f, dtype=F32)],
        [*normed, *low, *act, *branch, *biases],
        flops=4 * rows * d * f,
        in_specs=[HBM] * 8 + [VMEM] * 2,
        scratch=product_scratch(saved),
        after=after,
        **room(rows // 2, 24),
    )


def own_grads(layer, saved, biases, got, before, after=()):
    normed, low, act, branch = saved
    rows, d = sum(v.shape[0] for v in normed), normed[0].shape[1]
    f = low[0].shape[1] // 2
    return run(
        functools.partial(own_kernel, layer, len(before)),
        [shaped(2, d, f, dtype=F32), shaped(2, f, d, dtype=F32), shaped(1, f, dtype=F32)],
        [*normed, *low, *act, *branch, *biases, *got, *before],
        flops=4 * rows * d * f,
        in_specs=[HBM] * 8 + [VMEM] * 2 + [HBM] * 2 + [VMEM] + [HBM] * len(before),
        out_specs=[HBM, HBM, VMEM],
        scratch=[
            *product_scratch(saved),
            pltpu.VMEM((d, f), BF16),
            pltpu.VMEM((f, d), BF16),
            pltpu.VMEM((d, f), F32),
            pltpu.VMEM((f, d), F32),
            dma(2),
            dma(4),
        ],
        aliases={13 + k: k for k in range(len(before))},
        after=after,
        name=f"own_grads_sublayer{layer}",
        **room(rows // 2, 32),
    )


def expert_group(sizes, arrived, outgoing_g, target, tokens, grad_output, vectors, biases, weights):
    edge, window = sizes[0], sum(sizes)
    d, worst, senders = tokens.shape[1], arrived.shape[0], lax.axis_size("ex")
    exchange = functools.partial(lax.all_to_all, axis_name="ex", split_axis=0, concat_axis=0, tiled=True)
    one_hot_flops = 2 * window * worst * d

    def unpack(returned, values):
        return run(unpack_kernel, [shaped(*values.shape)], [target, returned, values], flops=one_hot_flops)[0]

    position = lax.axis_index("rep").astype(jnp.int32).reshape(1)
    x_own, place, count = run(
        functools.partial(place_kernel, senders, edge),
        [shaped(window, d), shaped(1, worst, dtype=jnp.int32), shaped(1, 128, dtype=F32)],
        [position, arrived],
        in_specs=[SMEM, VMEM],
        flops=one_hot_flops,
        name="place",
    )
    have = {"x_own": x_own, "x_far": swap(x_own, 2)}
    count_far = swap(count, 2)
    g_arrived = exchange(outgoing_g)

    *keep_e0, have["pE"] = forward(0, "E", sizes, have, vectors, biases, weights)
    have["qF"] = swap(have["pE"], 2)
    *keep_fw0, have["pFW"] = forward(0, "FW", sizes, have, vectors, biases, weights, (have["pE"],))
    have["qOW"] = swap(have["pFW"], 2)
    g_own = run(compact_kernel, [shaped(window, d)], [place, g_arrived], flops=one_hot_flops)[0]
    have["g_own"], have["g_far"] = g_own, swap(g_own, 2)

    *keep_f1, far1 = forward(1, "F", sizes, have, vectors, biases, weights)
    have["vE"] = swap(far1, 2)
    *keep_ow1, have["u"], shared1 = forward(1, "OW", sizes, have, vectors, biases, weights, send=True)
    have["vS"] = swap(shared1, 2)
    branch_ow1, low_ow1, have["dOW"], columns_ow1, bias_ow1 = backward(
        1, "OW", sizes, have, vectors, keep_ow1[2], weights
    )
    have["hFW"] = swap(have["dOW"], 2)
    branch_f1, low_f1, have["dF"], columns_f1, bias_f1 = backward(
        1, "F", sizes, have, vectors, keep_f1[2], weights, (bias_ow1,)
    )
    have["hE"] = swap(have["dF"], 2)

    names = list(dict.fromkeys([*names_of("OW", "x", "p", "q"), "u", "vE", "vS", "g_own"]))
    result, logit = run(
        functools.partial(result_kernel, senders, edge, names),
        [shaped(worst, d), shaped(window, 128, dtype=F32)],
        [*(have[k] for k in names), place, count, count_far, vectors],
        flops=one_hot_flops,
        name="result",
        after=(bias_ow1,),
        **room(window, 20),
    )
    returned = exchange(result)

    saved1 = (
        (keep_ow1[0], keep_f1[0]),
        (low_ow1, low_f1),
        (keep_ow1[1], keep_f1[1]),
        (branch_ow1, branch_f1),
    )
    biases1 = (bias_ow1, bias_f1)
    sent1 = sibling_grads(saved1, biases1)
    got1 = [swap(v, 1) for v in sent1]

    branch_fw0, low_fw0, have["cFW"], columns_fw0, bias_fw0, d_shared = backward(
        0, "FW", sizes, have, vectors, keep_fw0[2], weights, (sent1[2],)
    )
    got_c = swap(have["cFW"], 2)
    branch_e0, low_e0, have["cE"], columns_e0, bias_e0, d_edge = backward(
        0, "E", sizes, have, vectors, keep_e0[2], weights
    )
    saved0 = (
        (keep_e0[0], keep_fw0[0]),
        (low_e0, low_fw0),
        (keep_e0[1], keep_fw0[1]),
        (branch_e0, branch_fw0),
    )
    biases0 = (bias_e0, bias_fw0)
    sent0 = sibling_grads(saved0, biases0)
    names = names_of("OW", "x", "c")
    d_rows, columns_x = run(
        functools.partial(row_grad_kernel, edge, names),
        [shaped(worst, d), shaped(1, d, dtype=F32)],
        [*(have[k] for k in names), place, d_edge, d_shared, got_c, logit, vectors],
        flops=one_hot_flops,
        name="row_grad",
        after=(sent0[2],),
        **room(window, 20),
    )
    d_back = exchange(d_rows)

    grad_first, grad_second, grad_bias1 = own_grads(1, saved1, biases1, got1, (), (columns_x,))
    got0 = [swap(v, 1) for v in sent0]
    grad_first, grad_second, grad_bias0 = own_grads(
        0, saved0, biases0, got0, (grad_first, grad_second)
    )

    marks = run(functools.partial(marks_kernel, senders), [shaped(1, d, dtype=F32)], [returned], name="marks")[0]
    row_sums = [columns_x, columns_e0, columns_fw0, columns_ow1, columns_f1, marks]
    columns = run(columns_kernel, [shaped(8, d, dtype=F32)], row_sums)[0]
    columns = run(add_kernel, [shaped(8, d, dtype=F32)], [columns, swap(columns, 1)])[0]
    width = d // lax.axis_size("rep")
    *small, grad_bias, over = run(
        finish_kernel,
        [shaped(n, width, dtype=F32) for n in (1, 2, 2, 2)]
        + [shaped(2, grad_bias0.shape[1], dtype=F32), shaped(1, 128, dtype=F32)],
        [position, columns, swap(columns, 2), grad_bias0, grad_bias1],
        in_specs=[SMEM] + [VMEM] * 4,
    )
    outs = (
        unpack(returned, tokens),
        unpack(d_back, grad_output),
        small[0],
        small[1][None],
        small[2][None],
        grad_first[None],
        grad_bias[None],
        grad_second[None],
        small[3][None],
    )
    return outs, over[0, 0]


def shards(
    tokens, lengths, assign, centroids, ln_gain, ln_bias, w_in, b_in, w_out, b_out, grad_output
):
    experts, reps = lax.axis_size("ex"), lax.axis_size("rep")
    rows_here, d = tokens.shape
    slots = ceil_to(max(2, 5 * rows_here // (4 * experts)) + 1, 8)
    worst = experts * slots
    base = ((lax.axis_index("ex") * reps + lax.axis_index("rep")) * rows_here).astype(jnp.int32).reshape(1)
    target, outgoing = run(
        functools.partial(route_kernel, experts, slots),
        [shaped(1, rows_here, dtype=jnp.int32), shaped(worst, d)],
        [lengths, base, assign.reshape(1, rows_here), tokens],
        in_specs=[SMEM, SMEM, VMEM, VMEM],
        name="route",
        flops=2 * worst * rows_here * d,
    )
    arrived = lax.all_to_all(outgoing, "ex", split_axis=0, concat_axis=0, tiled=True)
    biases = (b_in[0], swap(b_in[0], 1))
    weights = (w_in[0], swap(w_in[0], 1), w_out[0], swap(w_out[0], 1))
    own_vectors = jnp.concatenate([centroids, ln_gain[0], ln_bias[0], b_out[0]], 0)
    own_vectors = jnp.concatenate([own_vectors, outgoing[:1, : own_vectors.shape[1]]], 0)
    vectors = lax.all_gather(own_vectors, "rep", axis=1, tiled=True).astype(F32)
    outgoing_g = run(
        pack_kernel,
        [shaped(worst, d)],
        [target, grad_output],
        flops=2 * worst * rows_here * d,
        after=(vectors,),
    )[0]

    operands = (arrived, outgoing_g, target, tokens, grad_output, vectors, biases, weights)
    most = ceil_to(experts * max(2, 5 * rows_here // (4 * experts)), 16)
    if EDGE + SHARED >= most:
        return expert_group((most, 16), *operands)[0]
    outs, over = expert_group((EDGE, SHARED), *operands)
    return lax.cond(over > 0.0, lambda *_: expert_group((most, 16), *operands)[0], lambda *kept: kept, *outs)


def solution(mesh):
    rows = P(("ex", "rep"), None)
    in_specs = (
        rows,
        P(),
        rows,
        P("ex", "rep"),
        P("ex", None, "rep"),
        P("ex", None, "rep"),
        P("ex", None, None, "rep"),
        P("ex", None, "rep"),
        P("ex", None, "rep", None),
        P("ex", None, "rep"),
        rows,
    )
    out_specs = (
        rows,
        rows,
        P("ex", "rep"),
        P("ex", None, "rep"),
        P("ex", None, "rep"),
        P("ex", None, None, "rep"),
        P("ex", None, "rep"),
        P("ex", None, "rep", None),
        P("ex", None, "rep"),
    )
    return jax.shard_map(shards, mesh=mesh, in_specs=in_specs, out_specs=out_specs, check_vma=False)
```

```python
import functools

import jax
import jax.numpy as jnp
from jax import lax
from jax.experimental import pallas as pl
from jax.experimental.pallas import tpu as pltpu
from jax.sharding import PartitionSpec as P

SEQ_LEN = 2048
EPSILON = 1e-05
F32 = jnp.float32
BF16 = jnp.bfloat16
VMEM = pl.BlockSpec(memory_space=pltpu.VMEM)
SMEM = pl.BlockSpec(memory_space=pltpu.SMEM)
ANY = pl.BlockSpec(memory_space=pl.ANY)
HBM = pl.BlockSpec(memory_space=pltpu.HBM)
EDGE, SHARED = 448, 192
TAIL = 16
SCALE = 16
COSTS = {(0, "E"): 128, (1, "F"): 48}


def swap(value, mask):
    return lax.ppermute(value, "rep", [(r, r ^ mask) for r in range(lax.axis_size("rep"))])


def dot(left, right, over_left, over_right):
    dims = (((over_left,), (over_right,)), ((), ()))
    return lax.dot_general(left, right, dims, preferred_element_type=F32)


def ceil_to(value, unit):
    return -(-value // unit) * unit


def shaped(*shape, dtype=BF16):
    return jax.ShapeDtypeStruct(shape, dtype)


def run(kernel, outs, operands, flops=0, scratch=(), in_specs=None, out_specs=None, limit=24, aliases=None, after=(), pinned=False, name=None):
    outs, count, extra = list(outs), len(operands), len(after)
    moved = sum(v.size * v.dtype.itemsize for v in (*operands, *outs))

    def body(*refs):
        kernel(*refs[:count], *refs[count + extra :])

    specs = in_specs or [VMEM] * count
    places = {id(HBM): pltpu.HBM, id(VMEM): pltpu.VMEM if pinned else pl.ANY}
    operands = [
        pltpu.with_memory_space_constraint(v, places.get(id(spec), pl.ANY))
        for v, spec in zip(operands, specs)
    ]
    out_specs = out_specs or [VMEM] * len(outs)
    outs = [
        pltpu.HBM(o.shape, o.dtype) if spec is HBM else o for o, spec in zip(outs, out_specs)
    ]
    return pl.pallas_call(
        body,
        out_shape=outs,
        in_specs=[*specs, *([ANY] * extra)],
        out_specs=out_specs,
        scratch_shapes=list(scratch),
        input_output_aliases=aliases or {},
        cost_estimate=pl.CostEstimate(flops=flops // SCALE, bytes_accessed=moved // SCALE, transcendentals=0),
        compiler_params=pltpu.CompilerParams(vmem_limit_bytes=limit << 20),
        name=name or kernel.__name__,
    )(*operands, *after)


def room(rows, limit):
    return dict(limit=limit, pinned=True) if rows <= 640 else dict(limit=54)


def iota(shape, dim):
    return lax.broadcasted_iota(jnp.int32, shape, dim)


def onehot(rows, index):
    return (iota((rows, index.shape[1]), 0) == index).astype(F32).astype(BF16)


def normalize(hidden):
    center = hidden - jnp.mean(hidden, -1, keepdims=True)
    rstd = lax.rsqrt(jnp.mean(center * center, -1, keepdims=True) + EPSILON)
    return center * rstd, rstd


def norm_backward(d_normed, xhat, rstd, gain):
    dx = d_normed * gain
    mean = jnp.mean(dx, -1, keepdims=True)
    return (dx - mean - xhat * jnp.mean(dx * xhat, -1, keepdims=True)) * rstd


def gelu_both(a):
    c = 0.7978845608028654
    a2 = a * a
    t = jnp.tanh(a * (c + (c * 0.044715) * a2))
    half = 0.5 + 0.5 * t
    act = a * half
    return act, half + act * (1.0 - t) * (c + (3 * c * 0.044715) * a2)


def gate_of(rows, centroid):
    return 1.0 / (1.0 + jnp.exp(-jnp.sum(rows * centroid, -1, keepdims=True)))


def up(ref):
    return ref[...].astype(F32)


CENTROID, GAIN, SHIFT, B_OUT = 0, 1, 3, 5


def row(ref, index):
    return ref[index : index + 1, :]


def route_kernel(experts, slots, lengths, base, assign, tokens, target_ref, packed_ref):
    n = assign.shape[1]
    position = base[0] + iota((1, n), 1)
    first = base[0] // SEQ_LEN
    limit = jnp.zeros((1, n), jnp.int32)
    for k in range(n // SEQ_LEN + 2):
        s = first + k
        size = lengths[jnp.minimum(s, lengths.shape[0] - 1)]
        within = position - s * SEQ_LEN
        limit = jnp.where((within >= 0) & (within < size), 1, limit)
    live = limit > 0
    expert = assign[...]
    hits = ((iota((experts, n), 0) == expert) & live).astype(F32)
    before = (iota((n, n), 0) < iota((n, n), 1)).astype(F32).astype(BF16)
    earlier = dot(hits.astype(BF16), before, 1, 0)
    slot = jnp.sum(hits * earlier, 0, keepdims=True).astype(jnp.int32)
    target = jnp.where(live, expert * slots + slot, -1)
    target_ref[...] = target
    packed = dot(onehot(experts * slots, target), tokens[...], 1, 0)
    packed_ref[...] = packed.astype(BF16)
    counts = jnp.broadcast_to(jnp.sum(hits, 1, keepdims=True), (experts, 128)).astype(BF16)
    last = iota((experts * slots, experts), 0) == iota((experts * slots, experts), 1) * slots + slots - 1
    marks = dot(last.astype(F32).astype(BF16), counts, 1, 0)
    packed_ref[:, 0:128] = (packed[:, 0:128] + marks).astype(BF16)


def pack_kernel(target, values, packed_ref):
    packed_ref[...] = dot(onehot(packed_ref.shape[0], target[...]), values[...], 1, 0).astype(BF16)


def marks_kernel(sources, returned, mark_ref):
    slots = returned.shape[0] // sources
    total = jnp.zeros((1, 128), F32)
    for k in range(sources):
        total = total + returned[(k + 1) * slots - 1 : (k + 1) * slots, 0:128].astype(F32)
    mark_ref[...] = jnp.zeros(mark_ref.shape, F32)
    mark_ref[:, 0:128] = total


def columns_kernel(column_x, own0, far0, own1, far1, mark, columns_ref):
    columns_ref[0:1, :] = column_x[...]
    columns_ref[1:2, :] = own0[0:1, :] + far0[0:1, :]
    columns_ref[2:3, :] = own1[0:1, :] + far1[0:1, :]
    columns_ref[3:4, :] = own0[1:2, :] + far0[1:2, :]
    columns_ref[4:5, :] = own1[1:2, :] + far1[1:2, :]
    columns_ref[5:6, :] = own0[2:3, :] + far0[2:3, :]
    columns_ref[6:7, :] = own1[2:3, :] + far1[2:3, :]
    columns_ref[7:8, :] = mark[...]


def add_kernel(left, right, out_ref):
    out_ref[...] = left[...] + right[...]


def finish_kernel(position, left, right, bias0, bias1, centroid_ref, gain_ref, shift_ref, out_ref, bias_ref, mark_ref):
    width = centroid_ref.shape[1]
    total = left[...] + right[...]
    mine = total[:, 0:width]
    for k in range(1, total.shape[1] // width):
        mine = jnp.where(position[0] == k, total[:, k * width : (k + 1) * width], mine)
    centroid_ref[...] = mine[0:1]
    gain_ref[...] = mine[1:3]
    shift_ref[...] = mine[3:5]
    out_ref[...] = mine[5:7]
    mark_ref[...] = total[7:8, 0:128]
    bias_ref[0:1, :] = bias0[...]
    bias_ref[1:2, :] = bias1[...]


def unpack_kernel(target, returned, values, out_ref):
    places = onehot(returned.shape[0], target[...])
    moved = dot(places, returned[...], 0, 0)
    alive = dot(places, jnp.ones((returned.shape[0], 128), BF16), 0, 0)[:, 0:1] > 0.5
    out_ref[...] = jnp.where(alive, up(values) + moved, 0.0).astype(BF16)


def compact_kernel(place, arrived, edge_ref, shared_ref):
    edge = edge_ref.shape[0]
    rows = dot(onehot(edge + shared_ref.shape[0], place[...]), arrived[...], 1, 0).astype(BF16)
    edge_ref[...] = rows[:edge]
    shared_ref[...] = rows[edge:]


def place_kernel(senders, edge, position, arrived, rows_ref, place_ref, count_ref):
    n, window = arrived.shape[0], rows_ref.shape[0] - TAIL
    slots = n // senders
    lane = iota((1, n), 1).astype(F32)
    place, total = jnp.full((1, n), -1.0, F32), jnp.zeros((1, 1), F32)
    for k in range(senders):
        count = arrived[(k + 1) * slots - 1 : (k + 1) * slots, 0:128].astype(F32)[:, 0:1]
        slot = lane - k * slots
        place = jnp.where((slot >= 0.0) & (slot < count), total + slot, place)
        total = total + count
    backwards = (place >= edge) & ((position[0] // 2) % 2 == 1)
    place = jnp.where(backwards, window + edge - 1 - place, place)
    place_ref[...] = place.astype(jnp.int32)
    count_ref[...] = jnp.broadcast_to(total, count_ref.shape)
    rows_ref[0:window, :] = dot(onehot(window, place_ref[...]), arrived[...], 1, 0).astype(BF16)
    beyond = jnp.clip(total - edge, 0.0, 255.0)
    rows_ref[window:, :] = jnp.broadcast_to(beyond, (TAIL, arrived.shape[1])).astype(BF16)


def spread(place, values, slots_ref):
    places = onehot(values.shape[0], place[...])
    slots_ref[...] = dot(places, values, 0, 0).astype(BF16)


FIELDS = {
    "p": ("pE", "pFW", "pFW"),
    "q": ("qOW", "qF", "qOW"),
    "d": ("dOW", "dF", "dOW"),
    "h": ("hE", "hFW", "hFW"),
    "c": ("cE", "cFW", "cFW"),
}


def names_of(rows, *fields):
    names = []
    for field in fields:
        if field == "g":
            names.append("gE_own" if rows in ("E", "OW") else "gE_far")
            names += ["gS_own", "gS_far"] if rows in ("OW", "FW") else []
            continue
        if field in FIELDS:
            own, far, shared = FIELDS[field]
        else:
            own, far, shared = field + "_own", field + "_far", None
        names.append(own if rows in ("E", "OW") else far)
        if rows in ("OW", "FW"):
            names += [shared] if shared else [own, far]
    return list(dict.fromkeys(names))


def values_of(rows, field, edge, refs):
    if field == "g":
        first = up(refs["gE_own" if rows in ("E", "OW") else "gE_far"])
        return first if rows in ("E", "F") else jnp.concatenate([first, up(refs["gS_own"]) + up(refs["gS_far"])], 0)
    if field in FIELDS:
        own, far, shared = FIELDS[field]
    else:
        own, far, shared = field + "_own", field + "_far", None
    first = refs[own if rows in ("E", "OW") else far]
    if rows in ("E", "F"):
        return first[0:edge, :].astype(F32)
    if shared:
        inner = refs[shared][edge:, :].astype(F32)
    else:
        inner = slice(edge, refs[own].shape[0] - TAIL)
        inner = refs[own][inner, :].astype(F32) + refs[far][inner, :].astype(F32)
    return jnp.concatenate([first[0:edge, :].astype(F32), inner], 0)


def hidden1_of(rows, edge, refs, vectors):
    parts = [values_of(rows, field, edge, refs) for field in ("x", "p", "q")]
    return parts[0] + parts[1] + parts[2] + row(vectors, B_OUT)


class Copies:
    def __init__(self, sems):
        self.sems, self.made = sems, []

    def start(self, source, target):
        copy = pltpu.make_async_copy(source, target, self.sems.at[len(self.made)])
        copy.start()
        self.made.append(copy)
        return copy

    def wait(self):
        for copy in self.made:
            copy.wait()


def fetch(layer, weights, order, buffer, sems):
    copies = [
        pltpu.make_async_copy(weights[k].at[layer], buffer.at[k], sems.at[k]) for k in range(4)
    ]
    copies[order[0]].start()
    copies[order[1]].start()
    left = list(order)

    def got(k):
        assert left.pop(0) == k
        copies[k].wait()
        if len(left) > 1:
            copies[left[1]].start()
        return buffer[k]

    return got


def dma(count):
    return pltpu.SemaphoreType.DMA((count,))


def weight_scratch(weights):
    return [pltpu.VMEM((4, *weights[0].shape[1:]), BF16), dma(4)]


def forward_kernel(layer, rows, edge, names, send, *refs):
    n = len(names)
    named, (vectors, biases_own, biases_sib) = dict(zip(names, refs[:n])), refs[n : n + 3]
    got = fetch(layer, refs[n + 3 : n + 7], (0, 2, 1, 3), *refs[-2:])
    normed_out, act_out, slope_out, out_ref = refs[n + 7 : n + 11]
    normed, act, slope, sems = refs[-6:-2]
    copies = Copies(sems)
    hidden = hidden1_of(rows, edge, named, vectors) if layer else values_of(rows, "x", edge, named)
    xhat, _ = normalize(hidden)
    normed[...] = (xhat * row(vectors, GAIN + layer) + row(vectors, SHIFT + layer)).astype(BF16)
    copies.start(normed, normed_out)
    total = None
    for q, bias in enumerate((biases_own, biases_sib)):
        pre = dot(normed[...], got(q), 1, 0) + row(bias, layer).astype(F32)
        columns = slice(q * pre.shape[1], (q + 1) * pre.shape[1])
        value, change = gelu_both(pre)
        act[:, columns] = value.astype(BF16)
        slope[:, columns] = change.astype(BF16)
        copies.start(act.at[:, columns], act_out.at[:, columns])
        copies.start(slope.at[:, columns], slope_out.at[:, columns])
        part = dot(act[:, columns], got(2 + q), 1, 0)
        total = part if total is None else total + part
    out_ref[...] = total.astype(BF16)
    if send:
        refs[n + 11][...] = out_ref[edge:, :]
    copies.wait()


def forward(layer, rows, sizes, named, vectors, biases, weights, after=(), send=False):
    edge, count = sizes[0], sizes[0] + (sizes[1] if rows in ("OW", "FW") else 0)
    names = names_of(rows, *(("x", "p", "q") if layer else ("x",)))
    d, f = vectors.shape[1], 2 * weights[0].shape[2]
    small = [*(named[k] for k in names), vectors, *biases]
    return run(
        functools.partial(forward_kernel, layer, rows, edge, names, send),
        [shaped(count, d), shaped(count, f), shaped(count, f), shaped(count, d)] + [shaped(sizes[1], d)] * send,
        [*small, *weights],
        flops=4 * count * d * f,
        in_specs=[VMEM] * len(small) + [HBM] * 4,
        out_specs=[HBM] * 3 + [VMEM] * (1 + send),
        scratch=[
            pltpu.VMEM((count, d), BF16),
            pltpu.VMEM((count, f), BF16),
            pltpu.VMEM((count, f), BF16),
            dma(5),
            *weight_scratch(weights),
        ],
        after=after,
        name=f"forward_sublayer{layer}_{rows}",
        **room(count, 26),
    )


def backward_kernel(layer, rows, edge, names, *refs):
    n = len(names)
    named, (vectors, slope_in) = dict(zip(names, refs[:n])), refs[n : n + 2]
    got = fetch(layer, refs[n + 2 : n + 6], (2, 0, 3, 1), *refs[-2:])
    branch_out, low_out, out_ref, columns_ref, bias_ref = refs[n + 6 : n + 11]
    branch, low, slope, sems, slope_sem = refs[-7:-2]
    copies = Copies(sems)
    slope_copy = pltpu.make_async_copy(slope_in, slope, slope_sem.at[0])
    slope_copy.start()
    x = values_of(rows, "x", edge, named)
    d_hidden = gate_of(x, row(vectors, CENTROID)) * values_of(rows, "g", edge, named)
    if layer == 0:
        xhat, rstd = normalize(hidden1_of(rows, edge, named, vectors))
        d_normed = values_of(rows, "d", edge, named) + values_of(rows, "h", edge, named)
        d_hidden = d_hidden + norm_backward(d_normed, xhat, rstd, row(vectors, GAIN + 1))
        refs[n + 11][...] = d_hidden if rows == "E" else d_hidden[edge:]
    branch[...] = d_hidden.astype(BF16)
    copies.start(branch, branch_out)
    own = jnp.zeros((1, d_hidden.shape[1]), F32)
    if rows in ("E", "OW"):
        own = own + jnp.sum(d_hidden[:edge], 0, keepdims=True)
    if rows in ("OW", "FW"):
        own = own + 0.5 * jnp.sum(d_hidden[edge:], 0, keepdims=True)
    columns_ref[2:3, :] = own
    total = None
    for q in range(2):
        d_act = dot(branch[...], got(2 + q), 1, 1)
        if q == 0:
            slope_copy.wait()
        columns = slice(q * d_act.shape[1], (q + 1) * d_act.shape[1])
        d_pre = d_act * slope[:, columns].astype(F32)
        bias_ref[:, columns] = jnp.sum(d_pre, 0, keepdims=True)
        low[:, columns] = d_pre.astype(BF16)
        copies.start(low.at[:, columns], low_out.at[:, columns])
        part = dot(low[:, columns], got(q), 1, 1)
        total = part if total is None else total + part
    out_ref[...] = total.astype(BF16)
    xhat, _ = normalize(hidden1_of(rows, edge, named, vectors) if layer else values_of(rows, "x", edge, named))
    columns_ref[0:1, :] = jnp.sum(total * xhat, 0, keepdims=True)
    columns_ref[1:2, :] = jnp.sum(total, 0, keepdims=True)
    copies.wait()


def backward(layer, rows, sizes, named, vectors, slope, weights, after=()):
    edge, count = sizes[0], sizes[0] + (sizes[1] if rows in ("OW", "FW") else 0)
    names = names_of(rows, *(("x", "g", "p", "q") if layer else ("x", "g", "p", "q", "d", "h")))
    d, f = vectors.shape[1], 2 * weights[0].shape[2]
    outs = [shaped(count, d), shaped(count, f), shaped(count, d), shaped(3, d, dtype=F32), shaped(1, f, dtype=F32)]
    if layer == 0:
        outs.append(shaped(edge if rows == "E" else sizes[1], d, dtype=F32))
    operands = [named[k] for k in names]
    return run(
        functools.partial(backward_kernel, layer, rows, edge, names),
        outs,
        [*operands, vectors, slope, *weights],
        flops=COSTS.get((layer, rows), 4) * count * d * f,
        in_specs=[VMEM] * (len(operands) + 1) + [HBM] * 5,
        out_specs=[HBM] * 2 + [VMEM] * (len(outs) - 2),
        scratch=[
            pltpu.VMEM((count, d), BF16),
            pltpu.VMEM((count, f), BF16),
            pltpu.VMEM((count, f), BF16),
            dma(3),
            dma(1),
            *weight_scratch(weights),
        ],
        after=after,
        name=f"backward_sublayer{layer}_{rows}",
        **room(count, 32),
    )


def result_kernel(senders, edge, names, *refs):
    named = dict(zip(names, refs))
    place, count, vectors, slots_ref, logit_ref = refs[len(names) :]
    gate = gate_of(values_of("OW", "x", edge, named), row(vectors, CENTROID))
    hidden = hidden1_of("OW", edge, named, vectors)
    hidden = hidden + up(named["u"]) + jnp.concatenate([up(named["vE"]), up(named["vS"])], 0) + row(vectors, B_OUT + 1)
    own_g = jnp.concatenate([up(named["gE_own"]), up(named["gS_own"])], 0)
    d_gate = jnp.sum(own_g * hidden, -1, keepdims=True)
    d_logit = (d_gate * gate * (1.0 - gate)).astype(BF16).astype(F32)
    logit_ref[...] = jnp.broadcast_to(d_logit, logit_ref.shape)
    spread(place, (gate * hidden).astype(BF16), slots_ref)
    window = logit_ref.shape[0]
    inner = sum(up(named[k])[window : window + 1, 0:128] for k in ("x_own", "x_far"))
    over = jnp.where((count[...] > window) | (inner > window - edge), 1.0, 0.0).astype(BF16)
    slots = slots_ref.shape[0] // senders
    for k in range(senders):
        slots_ref[(k + 1) * slots - 1 : (k + 1) * slots, 0:128] = over


def row_grad_kernel(edge, names, *refs):
    named = dict(zip(names, refs))
    place, edge_grad, shared_grad, got, logit, vectors, slots_ref, columns_ref = refs[len(names) :]
    x = values_of("OW", "x", edge, named)
    xhat, rstd = normalize(x)
    d_logit = logit[:, 0:1]
    d_normed = values_of("OW", "c", edge, named) + up(got)
    d_hidden = jnp.concatenate([edge_grad[...], shared_grad[...]], 0)
    d_hidden = d_hidden + norm_backward(d_normed, xhat, rstd, row(vectors, GAIN))
    d_row = d_hidden + d_logit * row(vectors, CENTROID)
    spread(place, d_row.astype(BF16), slots_ref)
    columns_ref[...] = jnp.sum(d_logit * x, 0, keepdims=True)


def products(q, sources, buffers, sems):
    width = sources[2].shape[1] // 2
    columns = slice(q * width, (q + 1) * width)
    wide = (2, 3, 4, 5)
    order = (0, 2, 1, 3, 4, 6, 5, 7)
    copies = {
        k: pltpu.make_async_copy(
            sources[k].at[:, columns] if k in wide else sources[k], buffers[k], sems.at[k]
        )
        for k in order
    }
    for k in order:
        copies[k].start()

    def got(k):
        if k in copies:
            copies.pop(k).wait()
        return buffers[k]

    def first(part):
        return sum(dot(got(k)[...], got(2 + k)[:, part], 0, 0) for k in range(2))

    def second(part):
        return sum(dot(got(4 + k)[:, part], got(6 + k)[...], 0, 0) for k in range(2))

    return first, second, width


def sibling_kernel(*refs):
    first_ref, second_ref, bias_ref = refs[10:13]
    first, second, width = products(1, refs[:8], refs[13:21], refs[21])
    half = width // 2
    parts = [slice(k * half, (k + 1) * half) for k in range(2)]
    for part in parts:
        first_ref[:, part] = first(part).astype(BF16)
    for part in parts:
        second_ref[part, :] = second(part).astype(BF16)
    bias_ref[...] = (refs[8][...] + refs[9][...])[:, width:]


def own_kernel(layer, n_before, *refs):
    got_first_in, got_second_in, got_bias = refs[10:13]
    refs_out = refs[13 + n_before :]
    first_out, second_out, bias_ref = refs_out[:3]
    first, second, width = products(0, refs[:8], refs_out[3:11], refs_out[11])
    got_first, got_second, buffer_first, buffer_second, sems_in, sems = refs_out[12:]
    copies_in = Copies(sems_in)
    copy_first = copies_in.start(got_first_in, got_first)
    copy_second = copies_in.start(got_second_in, got_second)
    half = width // 2
    parts = [slice(k * half, (k + 1) * half) for k in range(2)]
    copies = Copies(sems)
    for k, part in enumerate(parts):
        value = first(part)
        if k == 0:
            copy_first.wait()
        buffer_first[:, part] = value + got_first[:, part].astype(F32)
        copies.start(buffer_first.at[:, part], first_out.at[layer, :, part])
    for k, part in enumerate(parts):
        value = second(part)
        if k == 0:
            copy_second.wait()
        buffer_second[part, :] = value + got_second[part, :].astype(F32)
        copies.start(buffer_second.at[part, :], second_out.at[layer, part, :])
    bias_ref[...] = (refs[8][...] + refs[9][...])[:, :width] + got_bias[...]
    copies.wait()


def product_scratch(saved):
    d, f = saved[0][0].shape[1], saved[1][0].shape[1] // 2
    counts = [v.shape[0] for v in saved[0]] * 4
    return [pltpu.VMEM((m, n), BF16) for m, n in zip(counts, (d, d, f, f, f, f, d, d))] + [dma(8)]


def sibling_grads(saved, biases, after=()):
    normed, low, act, branch = saved
    rows, d = sum(v.shape[0] for v in normed), normed[0].shape[1]
    f = low[0].shape[1] // 2
    return run(
        sibling_kernel,
        [shaped(d, f), shaped(f, d), shaped(1, f, dtype=F32)],
        [*normed, *low, *act, *branch, *biases],
        flops=4 * rows * d * f,
        in_specs=[HBM] * 8 + [VMEM] * 2,
        scratch=product_scratch(saved),
        after=after,
        **room(rows // 2, 24),
    )


def own_grads(layer, saved, biases, got, before, after=()):
    normed, low, act, branch = saved
    rows, d = sum(v.shape[0] for v in normed), normed[0].shape[1]
    f = low[0].shape[1] // 2
    return run(
        functools.partial(own_kernel, layer, len(before)),
        [shaped(2, d, f, dtype=F32), shaped(2, f, d, dtype=F32), shaped(1, f, dtype=F32)],
        [*normed, *low, *act, *branch, *biases, *got, *before],
        flops=4 * rows * d * f,
        in_specs=[HBM] * 8 + [VMEM] * 2 + [HBM] * 2 + [VMEM] + [HBM] * len(before),
        out_specs=[HBM, HBM, VMEM],
        scratch=[
            *product_scratch(saved),
            pltpu.VMEM((d, f), BF16),
            pltpu.VMEM((f, d), BF16),
            pltpu.VMEM((d, f), F32),
            pltpu.VMEM((f, d), F32),
            dma(2),
            dma(4),
        ],
        aliases={13 + k: k for k in range(len(before))},
        after=after,
        name=f"own_grads_sublayer{layer}",
        **room(rows // 2, 32),
    )


def expert_group(sizes, arrived, outgoing_g, target, tokens, grad_output, vectors, biases, weights):
    edge, window = sizes[0], sum(sizes)
    d, worst, senders = tokens.shape[1], arrived.shape[0], lax.axis_size("ex")
    exchange = functools.partial(lax.all_to_all, axis_name="ex", split_axis=0, concat_axis=0, tiled=True)
    one_hot_flops = 2 * window * worst * d

    def unpack(returned, values):
        return run(unpack_kernel, [shaped(*values.shape)], [target, returned, values], flops=one_hot_flops)[0]

    position = lax.axis_index("rep").astype(jnp.int32).reshape(1)
    x_own, place, count = run(
        functools.partial(place_kernel, senders, edge),
        [shaped(window + TAIL, d), shaped(1, worst, dtype=jnp.int32), shaped(1, 128, dtype=F32)],
        [position, arrived],
        in_specs=[SMEM, VMEM],
        flops=one_hot_flops,
        name="place",
        after=(outgoing_g,),
    )
    have = {"x_own": x_own, "x_far": swap(x_own, 2)}
    g_arrived = exchange(outgoing_g)

    *keep_e0, have["pE"] = forward(0, "E", sizes, have, vectors, biases, weights)
    have["qF"] = swap(have["pE"], 2)
    *keep_fw0, have["pFW"] = forward(0, "FW", sizes, have, vectors, biases, weights, (have["pE"],))
    have["qOW"] = swap(have["pFW"], 2)

    *keep_f1, far1 = forward(1, "F", sizes, have, vectors, biases, weights)
    have["vE"] = swap(far1, 2)
    *keep_ow1, have["u"], shared1 = forward(1, "OW", sizes, have, vectors, biases, weights, send=True)
    have["vS"] = swap(shared1, 2)
    have["gE_own"], have["gS_own"] = run(
        compact_kernel,
        [shaped(edge, d), shaped(sizes[1], d)],
        [place, g_arrived],
        flops=one_hot_flops,
        after=(shared1,),
    )
    have["gS_far"] = swap(have["gS_own"], 2)
    have["gE_far"] = swap(have["gE_own"], 2)
    branch_ow1, low_ow1, have["dOW"], columns_ow1, bias_ow1 = backward(
        1, "OW", sizes, have, vectors, keep_ow1[2], weights
    )
    have["hFW"] = swap(have["dOW"], 2)
    branch_f1, low_f1, have["dF"], columns_f1, bias_f1 = backward(
        1, "F", sizes, have, vectors, keep_f1[2], weights, (bias_ow1,)
    )
    have["hE"] = swap(have["dF"], 2)

    names = list(dict.fromkeys([*names_of("OW", "x", "p", "q"), "u", "vE", "vS", "gE_own", "gS_own"]))
    result, logit = run(
        functools.partial(result_kernel, senders, edge, names),
        [shaped(worst, d), shaped(window, 128, dtype=F32)],
        [*(have[k] for k in names), place, count, vectors],
        flops=one_hot_flops,
        name="result",
        **room(window, 20),
    )
    returned = exchange(result)

    saved1 = (
        (keep_ow1[0], keep_f1[0]),
        (low_ow1, low_f1),
        (keep_ow1[1], keep_f1[1]),
        (branch_ow1, branch_f1),
    )
    biases1 = (bias_ow1, bias_f1)
    sent1 = sibling_grads(saved1, biases1)
    got1 = [swap(v, 1) for v in sent1]

    branch_fw0, low_fw0, have["cFW"], columns_fw0, bias_fw0, d_shared = backward(
        0, "FW", sizes, have, vectors, keep_fw0[2], weights, (sent1[2],)
    )
    got_c = swap(have["cFW"], 2)
    branch_e0, low_e0, have["cE"], columns_e0, bias_e0, d_edge = backward(
        0, "E", sizes, have, vectors, keep_e0[2], weights
    )
    saved0 = (
        (keep_e0[0], keep_fw0[0]),
        (low_e0, low_fw0),
        (keep_e0[1], keep_fw0[1]),
        (branch_e0, branch_fw0),
    )
    biases0 = (bias_e0, bias_fw0)
    sent0 = sibling_grads(saved0, biases0)
    names = names_of("OW", "x", "c")
    d_rows, columns_x = run(
        functools.partial(row_grad_kernel, edge, names),
        [shaped(worst, d), shaped(1, d, dtype=F32)],
        [*(have[k] for k in names), place, d_edge, d_shared, got_c, logit, vectors],
        flops=one_hot_flops,
        name="row_grad",
        after=(sent0[2],),
        **room(window, 20),
    )
    d_back = exchange(d_rows)

    grad_first, grad_second, grad_bias1 = own_grads(1, saved1, biases1, got1, (), (columns_x,))
    got0 = [swap(v, 1) for v in sent0]
    grad_first, grad_second, grad_bias0 = own_grads(
        0, saved0, biases0, got0, (grad_first, grad_second)
    )

    marks = run(functools.partial(marks_kernel, senders), [shaped(1, d, dtype=F32)], [returned], name="marks")[0]
    row_sums = [columns_x, columns_e0, columns_fw0, columns_ow1, columns_f1, marks]
    columns = run(columns_kernel, [shaped(8, d, dtype=F32)], row_sums)[0]
    columns = run(add_kernel, [shaped(8, d, dtype=F32)], [columns, swap(columns, 1)])[0]
    width = d // lax.axis_size("rep")
    *small, grad_bias, over = run(
        finish_kernel,
        [shaped(n, width, dtype=F32) for n in (1, 2, 2, 2)]
        + [shaped(2, grad_bias0.shape[1], dtype=F32), shaped(1, 128, dtype=F32)],
        [position, columns, swap(columns, 2), grad_bias0, grad_bias1],
        in_specs=[SMEM] + [VMEM] * 4,
    )
    outs = (
        unpack(returned, tokens),
        unpack(d_back, grad_output),
        small[0],
        small[1][None],
        small[2][None],
        grad_first[None],
        grad_bias[None],
        grad_second[None],
        small[3][None],
    )
    return outs, over[0, 0]


def shards(
    tokens, lengths, assign, centroids, ln_gain, ln_bias, w_in, b_in, w_out, b_out, grad_output
):
    experts, reps = lax.axis_size("ex"), lax.axis_size("rep")
    rows_here, d = tokens.shape
    slots = ceil_to(max(2, 5 * rows_here // (4 * experts)) + 1, 8)
    worst = experts * slots
    base = ((lax.axis_index("ex") * reps + lax.axis_index("rep")) * rows_here).astype(jnp.int32).reshape(1)
    target, outgoing = run(
        functools.partial(route_kernel, experts, slots),
        [shaped(1, rows_here, dtype=jnp.int32), shaped(worst, d)],
        [lengths, base, assign.reshape(1, rows_here), tokens],
        in_specs=[SMEM, SMEM, VMEM, VMEM],
        name="route",
        flops=2 * worst * rows_here * d,
    )
    arrived = lax.all_to_all(outgoing, "ex", split_axis=0, concat_axis=0, tiled=True)
    biases = (b_in[0], swap(b_in[0], 1))
    weights = (w_in[0], swap(w_in[0], 1), w_out[0], swap(w_out[0], 1))
    own_vectors = jnp.concatenate([centroids, ln_gain[0], ln_bias[0], b_out[0]], 0)
    own_vectors = jnp.concatenate([own_vectors, outgoing[:1, : own_vectors.shape[1]]], 0)
    vectors = lax.all_gather(own_vectors, "rep", axis=1, tiled=True).astype(F32)
    outgoing_g = run(
        pack_kernel,
        [shaped(worst, d)],
        [target, grad_output],
        flops=2 * worst * rows_here * d,
        after=(vectors,),
    )[0]

    operands = (arrived, outgoing_g, target, tokens, grad_output, vectors, biases, weights)
    most = ceil_to(experts * max(2, 5 * rows_here // (4 * experts)), 16)
    if EDGE + SHARED >= most:
        return expert_group((most, 16), *operands)[0]
    outs, over = expert_group((EDGE, SHARED), *operands)
    return lax.cond(over > 0.0, lambda *_: expert_group((most, 16), *operands)[0], lambda *kept: kept, *outs)


def solution(mesh):
    rows = P(("ex", "rep"), None)
    in_specs = (
        rows,
        P(),
        rows,
        P("ex", "rep"),
        P("ex", None, "rep"),
        P("ex", None, "rep"),
        P("ex", None, None, "rep"),
        P("ex", None, "rep"),
        P("ex", None, "rep", None),
        P("ex", None, "rep"),
        rows,
    )
    out_specs = (
        rows,
        rows,
        P("ex", "rep"),
        P("ex", None, "rep"),
        P("ex", None, "rep"),
        P("ex", None, None, "rep"),
        P("ex", None, "rep"),
        P("ex", None, "rep", None),
        P("ex", None, "rep"),
    )
    return jax.shard_map(shards, mesh=mesh, in_specs=in_specs, out_specs=out_specs, check_vma=False)
```

```python
import functools

import jax
import jax.numpy as jnp
from jax import lax
from jax.experimental import pallas as pl
from jax.experimental.pallas import tpu as pltpu
from jax.sharding import PartitionSpec as P

SEQ_LEN = 2048
EPSILON = 1e-05
F32 = jnp.float32
BF16 = jnp.bfloat16
VMEM = pl.BlockSpec(memory_space=pltpu.VMEM)
SMEM = pl.BlockSpec(memory_space=pltpu.SMEM)
ANY = pl.BlockSpec(memory_space=pl.ANY)
HBM = pl.BlockSpec(memory_space=pltpu.HBM)
EDGE, SHARED = 448, 192
TAIL = 16
SCALE = 16
COSTS = {(0, "E"): 128, (1, "F"): 48}


def swap(value, mask):
    return lax.ppermute(value, "rep", [(r, r ^ mask) for r in range(lax.axis_size("rep"))])


def dot(left, right, over_left, over_right):
    dims = (((over_left,), (over_right,)), ((), ()))
    return lax.dot_general(left, right, dims, preferred_element_type=F32)


def ceil_to(value, unit):
    return -(-value // unit) * unit


def shaped(*shape, dtype=BF16):
    return jax.ShapeDtypeStruct(shape, dtype)


def run(kernel, outs, operands, flops=0, scratch=(), in_specs=None, out_specs=None, limit=24, aliases=None, after=(), pinned=False, name=None):
    outs, count, extra = list(outs), len(operands), len(after)
    moved = sum(v.size * v.dtype.itemsize for v in (*operands, *outs))

    def body(*refs):
        kernel(*refs[:count], *refs[count + extra :])

    specs = in_specs or [VMEM] * count
    places = {id(HBM): pltpu.HBM, id(VMEM): pltpu.VMEM if pinned else pl.ANY}
    operands = [
        pltpu.with_memory_space_constraint(v, places.get(id(spec), pl.ANY))
        for v, spec in zip(operands, specs)
    ]
    out_specs = out_specs or [VMEM] * len(outs)
    outs = [
        pltpu.HBM(o.shape, o.dtype) if spec is HBM else o for o, spec in zip(outs, out_specs)
    ]
    return pl.pallas_call(
        body,
        out_shape=outs,
        in_specs=[*specs, *([ANY] * extra)],
        out_specs=out_specs,
        scratch_shapes=list(scratch),
        input_output_aliases=aliases or {},
        cost_estimate=pl.CostEstimate(flops=flops // SCALE, bytes_accessed=moved // SCALE, transcendentals=0),
        compiler_params=pltpu.CompilerParams(vmem_limit_bytes=limit << 20),
        name=name or kernel.__name__,
    )(*operands, *after)


def room(rows, limit):
    return dict(limit=limit, pinned=True) if rows <= 640 else dict(limit=54)


def iota(shape, dim):
    return lax.broadcasted_iota(jnp.int32, shape, dim)


def onehot(rows, index):
    return (iota((rows, index.shape[1]), 0) == index).astype(F32).astype(BF16)


def normalize(hidden):
    center = hidden - jnp.mean(hidden, -1, keepdims=True)
    rstd = lax.rsqrt(jnp.mean(center * center, -1, keepdims=True) + EPSILON)
    return center * rstd, rstd


def norm_backward(d_normed, xhat, rstd, gain):
    dx = d_normed * gain
    mean = jnp.mean(dx, -1, keepdims=True)
    return (dx - mean - xhat * jnp.mean(dx * xhat, -1, keepdims=True)) * rstd


def gelu_both(a):
    c = 0.7978845608028654
    a2 = a * a
    t = jnp.tanh(a * (c + (c * 0.044715) * a2))
    half = 0.5 + 0.5 * t
    act = a * half
    return act, half + act * (1.0 - t) * (c + (3 * c * 0.044715) * a2)


def gate_of(rows, centroid):
    return 1.0 / (1.0 + jnp.exp(-jnp.sum(rows * centroid, -1, keepdims=True)))


def up(ref):
    return ref[...].astype(F32)


CENTROID, GAIN, SHIFT, B_OUT = 0, 1, 3, 5


def row(ref, index):
    return ref[index : index + 1, :]


def route_kernel(experts, slots, lengths, base, assign, tokens, target_ref, packed_ref):
    n = assign.shape[1]
    position = base[0] + iota((1, n), 1)
    first = base[0] // SEQ_LEN
    limit = jnp.zeros((1, n), jnp.int32)
    for k in range(n // SEQ_LEN + 2):
        s = first + k
        size = lengths[jnp.minimum(s, lengths.shape[0] - 1)]
        within = position - s * SEQ_LEN
        limit = jnp.where((within >= 0) & (within < size), 1, limit)
    live = limit > 0
    expert = assign[...]
    hits = ((iota((experts, n), 0) == expert) & live).astype(F32)
    before = (iota((n, n), 0) < iota((n, n), 1)).astype(F32).astype(BF16)
    earlier = dot(hits.astype(BF16), before, 1, 0)
    slot = jnp.sum(hits * earlier, 0, keepdims=True).astype(jnp.int32)
    target = jnp.where(live, expert * slots + slot, -1)
    target_ref[...] = target
    packed = dot(onehot(experts * slots, target), tokens[...], 1, 0)
    packed_ref[...] = packed.astype(BF16)
    counts = jnp.broadcast_to(jnp.sum(hits, 1, keepdims=True), (experts, 128)).astype(BF16)
    last = iota((experts * slots, experts), 0) == iota((experts * slots, experts), 1) * slots + slots - 1
    marks = dot(last.astype(F32).astype(BF16), counts, 1, 0)
    packed_ref[:, 0:128] = (packed[:, 0:128] + marks).astype(BF16)


def pack_kernel(target, values, packed_ref):
    packed_ref[...] = dot(onehot(packed_ref.shape[0], target[...]), values[...], 1, 0).astype(BF16)


def marks_kernel(sources, returned, mark_ref):
    slots = returned.shape[0] // sources
    total = jnp.zeros((1, 128), F32)
    for k in range(sources):
        total = total + returned[(k + 1) * slots - 1 : (k + 1) * slots, 0:128].astype(F32)
    mark_ref[...] = jnp.zeros(mark_ref.shape, F32)
    mark_ref[:, 0:128] = total


def columns_kernel(column_x, own0, far0, own1, far1, mark, columns_ref):
    columns_ref[0:1, :] = column_x[...]
    columns_ref[1:2, :] = own0[0:1, :] + far0[0:1, :]
    columns_ref[2:3, :] = own1[0:1, :] + far1[0:1, :]
    columns_ref[3:4, :] = own0[1:2, :] + far0[1:2, :]
    columns_ref[4:5, :] = own1[1:2, :] + far1[1:2, :]
    columns_ref[5:6, :] = own0[2:3, :] + far0[2:3, :]
    columns_ref[6:7, :] = own1[2:3, :] + far1[2:3, :]
    columns_ref[7:8, :] = mark[...]


def add_kernel(left, right, out_ref):
    out_ref[...] = left[...] + right[...]


def finish_kernel(position, left, right, bias0, bias1, centroid_ref, gain_ref, shift_ref, out_ref, bias_ref, mark_ref):
    width = centroid_ref.shape[1]
    total = left[...] + right[...]
    mine = total[:, 0:width]
    for k in range(1, total.shape[1] // width):
        mine = jnp.where(position[0] == k, total[:, k * width : (k + 1) * width], mine)
    centroid_ref[...] = mine[0:1]
    gain_ref[...] = mine[1:3]
    shift_ref[...] = mine[3:5]
    out_ref[...] = mine[5:7]
    mark_ref[...] = total[7:8, 0:128]
    bias_ref[0:1, :] = bias0[...]
    bias_ref[1:2, :] = bias1[...]


def unpack_kernel(target, returned, values, out_ref):
    places = onehot(returned.shape[0], target[...])
    moved = dot(places, returned[...], 0, 0)
    alive = dot(places, jnp.ones((returned.shape[0], 128), BF16), 0, 0)[:, 0:1] > 0.5
    out_ref[...] = jnp.where(alive, up(values) + moved, 0.0).astype(BF16)


def compact_kernel(place, arrived, edge_ref, shared_ref):
    edge = edge_ref.shape[0]
    rows = dot(onehot(edge + shared_ref.shape[0], place[...]), arrived[...], 1, 0).astype(BF16)
    edge_ref[...] = rows[:edge]
    shared_ref[...] = rows[edge:]


def place_kernel(senders, edge, position, arrived, rows_ref, place_ref, count_ref):
    n, window = arrived.shape[0], rows_ref.shape[0] - TAIL
    slots = n // senders
    lane = iota((1, n), 1).astype(F32)
    place, total = jnp.full((1, n), -1.0, F32), jnp.zeros((1, 1), F32)
    for k in range(senders):
        count = arrived[(k + 1) * slots - 1 : (k + 1) * slots, 0:128].astype(F32)[:, 0:1]
        slot = lane - k * slots
        place = jnp.where((slot >= 0.0) & (slot < count), total + slot, place)
        total = total + count
    backwards = (place >= edge) & ((position[0] // 2) % 2 == 1)
    place = jnp.where(backwards, window + edge - 1 - place, place)
    place_ref[...] = place.astype(jnp.int32)
    count_ref[...] = jnp.broadcast_to(total, count_ref.shape)
    rows_ref[0:window, :] = dot(onehot(window, place_ref[...]), arrived[...], 1, 0).astype(BF16)
    beyond = jnp.clip(total - edge, 0.0, 255.0)
    rows_ref[window:, :] = jnp.broadcast_to(beyond, (TAIL, arrived.shape[1])).astype(BF16)


def spread(place, values, slots_ref):
    places = onehot(values.shape[0], place[...])
    slots_ref[...] = dot(places, values, 0, 0).astype(BF16)


FIELDS = {
    "p": ("pE", "pFW", "pFW"),
    "q": ("qOW", "qF", "qOW"),
    "d": ("dOW", "dF", "dOW"),
    "h": ("hE", "hFW", "hFW"),
    "c": ("cE", "cFW", "cFW"),
}


def names_of(rows, *fields):
    names = []
    for field in fields:
        if field == "g":
            names.append("gE_own" if rows in ("E", "OW") else "gE_far")
            names += ["gS_own", "gS_far"] if rows in ("OW", "FW") else []
            continue
        if field in FIELDS:
            own, far, shared = FIELDS[field]
        else:
            own, far, shared = field + "_own", field + "_far", None
        names.append(own if rows in ("E", "OW") else far)
        if rows in ("OW", "FW"):
            names += [shared] if shared else [own, far]
    return list(dict.fromkeys(names))


def values_of(rows, field, edge, refs):
    if field == "g":
        first = up(refs["gE_own" if rows in ("E", "OW") else "gE_far"])
        return first if rows in ("E", "F") else jnp.concatenate([first, up(refs["gS_own"]) + up(refs["gS_far"])], 0)
    if field in FIELDS:
        own, far, shared = FIELDS[field]
    else:
        own, far, shared = field + "_own", field + "_far", None
    first = refs[own if rows in ("E", "OW") else far]
    if rows in ("E", "F"):
        return first[0:edge, :].astype(F32)
    if shared:
        inner = refs[shared][edge:, :].astype(F32)
    else:
        inner = slice(edge, refs[own].shape[0] - TAIL)
        inner = refs[own][inner, :].astype(F32) + refs[far][inner, :].astype(F32)
    return jnp.concatenate([first[0:edge, :].astype(F32), inner], 0)


def hidden1_of(rows, edge, refs, vectors):
    parts = [values_of(rows, field, edge, refs) for field in ("x", "p", "q")]
    return parts[0] + parts[1] + parts[2] + row(vectors, B_OUT)


class Copies:
    def __init__(self, sems):
        self.sems, self.made = sems, []

    def start(self, source, target):
        copy = pltpu.make_async_copy(source, target, self.sems.at[len(self.made)])
        copy.start()
        self.made.append(copy)
        return copy

    def wait(self):
        for copy in self.made:
            copy.wait()


def fetch(layer, weights, order, buffer, sems):
    copies = [
        pltpu.make_async_copy(weights[k].at[layer], buffer.at[k], sems.at[k]) for k in range(4)
    ]
    copies[order[0]].start()
    copies[order[1]].start()
    left = list(order)

    def got(k):
        assert left.pop(0) == k
        copies[k].wait()
        if len(left) > 1:
            copies[left[1]].start()
        return buffer[k]

    return got


def dma(count):
    return pltpu.SemaphoreType.DMA((count,))


def weight_scratch(weights):
    return [pltpu.VMEM((4, *weights[0].shape[1:]), BF16), dma(4)]


def forward_kernel(layer, rows, edge, names, send, *refs):
    n = len(names)
    named, (vectors, biases_own, biases_sib) = dict(zip(names, refs[:n])), refs[n : n + 3]
    got = fetch(layer, refs[n + 3 : n + 7], (0, 2, 1, 3), *refs[-2:])
    normed_out, act_out, slope_out, out_ref = refs[n + 7 : n + 11]
    normed, act, slope, sems = refs[-6:-2]
    copies = Copies(sems)
    hidden = hidden1_of(rows, edge, named, vectors) if layer else values_of(rows, "x", edge, named)
    xhat, _ = normalize(hidden)
    normed[...] = (xhat * row(vectors, GAIN + layer) + row(vectors, SHIFT + layer)).astype(BF16)
    copies.start(normed, normed_out)
    total = None
    for q, bias in enumerate((biases_own, biases_sib)):
        pre = dot(normed[...], got(q), 1, 0) + row(bias, layer).astype(F32)
        columns = slice(q * pre.shape[1], (q + 1) * pre.shape[1])
        value, change = gelu_both(pre)
        act[:, columns] = value.astype(BF16)
        slope[:, columns] = change.astype(BF16)
        copies.start(act.at[:, columns], act_out.at[:, columns])
        copies.start(slope.at[:, columns], slope_out.at[:, columns])
        part = dot(act[:, columns], got(2 + q), 1, 0)
        total = part if total is None else total + part
    out_ref[...] = total.astype(BF16)
    if send:
        refs[n + 11][...] = out_ref[edge:, :]
    copies.wait()


def forward(layer, rows, sizes, named, vectors, biases, weights, after=(), send=False):
    edge, count = sizes[0], sizes[0] + (sizes[1] if rows in ("OW", "FW") else 0)
    names = names_of(rows, *(("x", "p", "q") if layer else ("x",)))
    d, f = vectors.shape[1], 2 * weights[0].shape[2]
    small = [*(named[k] for k in names), vectors, *biases]
    return run(
        functools.partial(forward_kernel, layer, rows, edge, names, send),
        [shaped(count, d), shaped(count, f), shaped(count, f), shaped(count, d)] + [shaped(sizes[1], d)] * send,
        [*small, *weights],
        flops=4 * count * d * f,
        in_specs=[VMEM] * len(small) + [HBM] * 4,
        out_specs=[HBM] * 3 + [VMEM] * (1 + send),
        scratch=[
            pltpu.VMEM((count, d), BF16),
            pltpu.VMEM((count, f), BF16),
            pltpu.VMEM((count, f), BF16),
            dma(5),
            *weight_scratch(weights),
        ],
        after=after,
        name=f"forward_sublayer{layer}_{rows}",
        **room(count, 26),
    )


def backward_kernel(layer, rows, edge, names, *refs):
    n = len(names)
    named, (vectors, slope_in) = dict(zip(names, refs[:n])), refs[n : n + 2]
    got = fetch(layer, refs[n + 2 : n + 6], (2, 0, 3, 1), *refs[-2:])
    branch_out, low_out, out_ref, columns_ref, bias_ref = refs[n + 6 : n + 11]
    branch, low, slope, sems, slope_sem = refs[-7:-2]
    copies = Copies(sems)
    slope_copy = pltpu.make_async_copy(slope_in, slope, slope_sem.at[0])
    slope_copy.start()
    x = values_of(rows, "x", edge, named)
    d_hidden = gate_of(x, row(vectors, CENTROID)) * values_of(rows, "g", edge, named)
    if layer == 0:
        xhat, rstd = normalize(hidden1_of(rows, edge, named, vectors))
        d_normed = values_of(rows, "d", edge, named) + values_of(rows, "h", edge, named)
        d_hidden = d_hidden + norm_backward(d_normed, xhat, rstd, row(vectors, GAIN + 1))
        refs[n + 11][...] = d_hidden if rows == "E" else d_hidden[edge:]
    branch[...] = d_hidden.astype(BF16)
    copies.start(branch, branch_out)
    own = jnp.zeros((1, d_hidden.shape[1]), F32)
    if rows in ("E", "OW"):
        own = own + jnp.sum(d_hidden[:edge], 0, keepdims=True)
    if rows in ("OW", "FW"):
        own = own + 0.5 * jnp.sum(d_hidden[edge:], 0, keepdims=True)
    columns_ref[2:3, :] = own
    total = None
    for q in range(2):
        d_act = dot(branch[...], got(2 + q), 1, 1)
        if q == 0:
            slope_copy.wait()
        columns = slice(q * d_act.shape[1], (q + 1) * d_act.shape[1])
        d_pre = d_act * slope[:, columns].astype(F32)
        bias_ref[:, columns] = jnp.sum(d_pre, 0, keepdims=True)
        low[:, columns] = d_pre.astype(BF16)
        copies.start(low.at[:, columns], low_out.at[:, columns])
        part = dot(low[:, columns], got(q), 1, 1)
        total = part if total is None else total + part
    out_ref[...] = total.astype(BF16)
    xhat, _ = normalize(hidden1_of(rows, edge, named, vectors) if layer else values_of(rows, "x", edge, named))
    columns_ref[0:1, :] = jnp.sum(total * xhat, 0, keepdims=True)
    columns_ref[1:2, :] = jnp.sum(total, 0, keepdims=True)
    copies.wait()


def backward(layer, rows, sizes, named, vectors, slope, weights, after=()):
    edge, count = sizes[0], sizes[0] + (sizes[1] if rows in ("OW", "FW") else 0)
    names = names_of(rows, *(("x", "g", "p", "q") if layer else ("x", "g", "p", "q", "d", "h")))
    d, f = vectors.shape[1], 2 * weights[0].shape[2]
    outs = [shaped(count, d), shaped(count, f), shaped(count, d), shaped(3, d, dtype=F32), shaped(1, f, dtype=F32)]
    if layer == 0:
        outs.append(shaped(edge if rows == "E" else sizes[1], d, dtype=F32))
    operands = [named[k] for k in names]
    return run(
        functools.partial(backward_kernel, layer, rows, edge, names),
        outs,
        [*operands, vectors, slope, *weights],
        flops=COSTS.get((layer, rows), 4) * count * d * f,
        in_specs=[VMEM] * (len(operands) + 1) + [HBM] * 5,
        out_specs=[HBM] * 2 + [VMEM] * (len(outs) - 2),
        scratch=[
            pltpu.VMEM((count, d), BF16),
            pltpu.VMEM((count, f), BF16),
            pltpu.VMEM((count, f), BF16),
            dma(3),
            dma(1),
            *weight_scratch(weights),
        ],
        after=after,
        name=f"backward_sublayer{layer}_{rows}",
        **room(count, 32),
    )


def result_kernel(senders, edge, names, *refs):
    named = dict(zip(names, refs))
    place, count, vectors, slots_ref, logit_ref = refs[len(names) :]
    gate = gate_of(values_of("OW", "x", edge, named), row(vectors, CENTROID))
    hidden = hidden1_of("OW", edge, named, vectors)
    hidden = hidden + up(named["u"]) + jnp.concatenate([up(named["vE"]), up(named["vS"])], 0) + row(vectors, B_OUT + 1)
    own_g = jnp.concatenate([up(named["gE_own"]), up(named["gS_own"])], 0)
    d_gate = jnp.sum(own_g * hidden, -1, keepdims=True)
    d_logit = (d_gate * gate * (1.0 - gate)).astype(BF16).astype(F32)
    logit_ref[...] = jnp.broadcast_to(d_logit, logit_ref.shape)
    spread(place, (gate * hidden).astype(BF16), slots_ref)
    window = logit_ref.shape[0]
    inner = sum(up(named[k])[window : window + 1, 0:128] for k in ("x_own", "x_far"))
    over = jnp.where((count[...] > window) | (inner > window - edge), 1.0, 0.0).astype(BF16)
    slots = slots_ref.shape[0] // senders
    for k in range(senders):
        slots_ref[(k + 1) * slots - 1 : (k + 1) * slots, 0:128] = over


def row_grad_kernel(edge, names, *refs):
    named = dict(zip(names, refs))
    place, edge_grad, shared_grad, got, logit, vectors, slots_ref, columns_ref = refs[len(names) :]
    x = values_of("OW", "x", edge, named)
    xhat, rstd = normalize(x)
    d_logit = logit[:, 0:1]
    d_normed = values_of("OW", "c", edge, named) + up(got)
    d_hidden = jnp.concatenate([edge_grad[...], shared_grad[...]], 0)
    d_hidden = d_hidden + norm_backward(d_normed, xhat, rstd, row(vectors, GAIN))
    d_row = d_hidden + d_logit * row(vectors, CENTROID)
    spread(place, d_row.astype(BF16), slots_ref)
    columns_ref[...] = jnp.sum(d_logit * x, 0, keepdims=True)


def products(q, sources, buffers, sems):
    width = sources[2].shape[1] // 2
    columns = slice(q * width, (q + 1) * width)
    wide = (2, 3, 4, 5)
    order = (0, 2, 1, 3, 4, 6, 5, 7)
    copies = {
        k: pltpu.make_async_copy(
            sources[k].at[:, columns] if k in wide else sources[k], buffers[k], sems.at[k]
        )
        for k in order
    }
    for k in order:
        copies[k].start()

    def got(k):
        if k in copies:
            copies.pop(k).wait()
        return buffers[k]

    def first(part):
        return sum(dot(got(k)[...], got(2 + k)[:, part], 0, 0) for k in range(2))

    def second(part):
        return sum(dot(got(4 + k)[:, part], got(6 + k)[...], 0, 0) for k in range(2))

    return first, second, width


def sibling_kernel(*refs):
    first_ref, second_ref, bias_ref = refs[10:13]
    first, second, width = products(1, refs[:8], refs[13:21], refs[21])
    half = width // 2
    parts = [slice(k * half, (k + 1) * half) for k in range(2)]
    for part in parts:
        first_ref[:, part] = first(part).astype(BF16)
    for part in parts:
        second_ref[part, :] = second(part).astype(BF16)
    bias_ref[...] = (refs[8][...] + refs[9][...])[:, width:]


def own_kernel(layer, n_before, *refs):
    got_first_in, got_second_in, got_bias = refs[10:13]
    refs_out = refs[13 + n_before :]
    first_out, second_out, bias_ref = refs_out[:3]
    first, second, width = products(0, refs[:8], refs_out[3:11], refs_out[11])
    got_first, got_second, buffer_first, buffer_second, sems_in, sems = refs_out[12:]
    copies_in = Copies(sems_in)
    copy_first = copies_in.start(got_first_in, got_first)
    copy_second = copies_in.start(got_second_in, got_second)
    half = width // 2
    parts = [slice(k * half, (k + 1) * half) for k in range(2)]
    copies = Copies(sems)
    for k, part in enumerate(parts):
        value = first(part)
        if k == 0:
            copy_first.wait()
        buffer_first[:, part] = value + got_first[:, part].astype(F32)
        copies.start(buffer_first.at[:, part], first_out.at[layer, :, part])
    for k, part in enumerate(parts):
        value = second(part)
        if k == 0:
            copy_second.wait()
        buffer_second[part, :] = value + got_second[part, :].astype(F32)
        copies.start(buffer_second.at[part, :], second_out.at[layer, part, :])
    bias_ref[...] = (refs[8][...] + refs[9][...])[:, :width] + got_bias[...]
    copies.wait()


def product_scratch(saved):
    d, f = saved[0][0].shape[1], saved[1][0].shape[1] // 2
    counts = [v.shape[0] for v in saved[0]] * 4
    return [pltpu.VMEM((m, n), BF16) for m, n in zip(counts, (d, d, f, f, f, f, d, d))] + [dma(8)]


def sibling_grads(saved, biases, after=()):
    normed, low, act, branch = saved
    rows, d = sum(v.shape[0] for v in normed), normed[0].shape[1]
    f = low[0].shape[1] // 2
    return run(
        sibling_kernel,
        [shaped(d, f), shaped(f, d), shaped(1, f, dtype=F32)],
        [*normed, *low, *act, *branch, *biases],
        flops=4 * rows * d * f,
        in_specs=[HBM] * 8 + [VMEM] * 2,
        scratch=product_scratch(saved),
        after=after,
        **room(rows // 2, 24),
    )


def own_grads(layer, saved, biases, got, before, after=()):
    normed, low, act, branch = saved
    rows, d = sum(v.shape[0] for v in normed), normed[0].shape[1]
    f = low[0].shape[1] // 2
    return run(
        functools.partial(own_kernel, layer, len(before)),
        [shaped(2, d, f, dtype=F32), shaped(2, f, d, dtype=F32), shaped(1, f, dtype=F32)],
        [*normed, *low, *act, *branch, *biases, *got, *before],
        flops=4 * rows * d * f,
        in_specs=[HBM] * 8 + [VMEM] * 2 + [HBM] * 2 + [VMEM] + [HBM] * len(before),
        out_specs=[HBM, HBM, VMEM],
        scratch=[
            *product_scratch(saved),
            pltpu.VMEM((d, f), BF16),
            pltpu.VMEM((f, d), BF16),
            pltpu.VMEM((d, f), F32),
            pltpu.VMEM((f, d), F32),
            dma(2),
            dma(4),
        ],
        aliases={13 + k: k for k in range(len(before))},
        after=after,
        name=f"own_grads_sublayer{layer}",
        **room(rows // 2, 32),
    )


def expert_group(sizes, arrived, outgoing_g, target, tokens, grad_output, vectors, biases, weights):
    edge, window = sizes[0], sum(sizes)
    d, worst, senders = tokens.shape[1], arrived.shape[0], lax.axis_size("ex")
    exchange = functools.partial(lax.all_to_all, axis_name="ex", split_axis=0, concat_axis=0, tiled=True)
    one_hot_flops = 2 * window * worst * d

    def unpack(returned, values):
        return run(unpack_kernel, [shaped(*values.shape)], [target, returned, values], flops=one_hot_flops)[0]

    position = lax.axis_index("rep").astype(jnp.int32).reshape(1)
    x_own, place, count = run(
        functools.partial(place_kernel, senders, edge),
        [shaped(window + TAIL, d), shaped(1, worst, dtype=jnp.int32), shaped(1, 128, dtype=F32)],
        [position, arrived],
        in_specs=[SMEM, VMEM],
        flops=one_hot_flops,
        name="place",
        after=(outgoing_g,),
    )
    have = {"x_own": x_own, "x_far": swap(x_own, 2)}
    g_arrived = exchange(outgoing_g)

    *keep_e0, have["pE"] = forward(0, "E", sizes, have, vectors, biases, weights)
    have["qF"] = swap(have["pE"], 2)
    *keep_fw0, have["pFW"] = forward(0, "FW", sizes, have, vectors, biases, weights, (have["pE"],))
    have["qOW"] = swap(have["pFW"], 2)

    *keep_f1, far1 = forward(1, "F", sizes, have, vectors, biases, weights)
    have["vE"] = swap(far1, 2)
    *keep_ow1, have["u"], shared1 = forward(1, "OW", sizes, have, vectors, biases, weights, send=True)
    have["vS"] = swap(shared1, 2)
    have["gE_own"], have["gS_own"] = run(
        compact_kernel,
        [shaped(edge, d), shaped(sizes[1], d)],
        [place, g_arrived],
        flops=one_hot_flops,
        after=(shared1,),
    )
    have["gS_far"] = swap(have["gS_own"], 2)
    have["gE_far"] = swap(have["gE_own"], 2)
    branch_ow1, low_ow1, have["dOW"], columns_ow1, bias_ow1 = backward(
        1, "OW", sizes, have, vectors, keep_ow1[2], weights
    )
    have["hFW"] = swap(have["dOW"], 2)
    branch_f1, low_f1, have["dF"], columns_f1, bias_f1 = backward(
        1, "F", sizes, have, vectors, keep_f1[2], weights, (bias_ow1,)
    )
    have["hE"] = swap(have["dF"], 2)

    names = list(dict.fromkeys([*names_of("OW", "x", "p", "q"), "u", "vE", "vS", "gE_own", "gS_own"]))
    result, logit = run(
        functools.partial(result_kernel, senders, edge, names),
        [shaped(worst, d), shaped(window, 128, dtype=F32)],
        [*(have[k] for k in names), place, count, vectors],
        flops=one_hot_flops,
        name="result",
        **room(window, 20),
    )
    returned = exchange(result)

    saved1 = (
        (keep_ow1[0], keep_f1[0]),
        (low_ow1, low_f1),
        (keep_ow1[1], keep_f1[1]),
        (branch_ow1, branch_f1),
    )
    biases1 = (bias_ow1, bias_f1)
    sent1 = sibling_grads(saved1, biases1)
    got1 = [swap(v, 1) for v in sent1]

    branch_fw0, low_fw0, have["cFW"], columns_fw0, bias_fw0, d_shared = backward(
        0, "FW", sizes, have, vectors, keep_fw0[2], weights, (sent1[2],)
    )
    got_c = swap(have["cFW"], 2)
    branch_e0, low_e0, have["cE"], columns_e0, bias_e0, d_edge = backward(
        0, "E", sizes, have, vectors, keep_e0[2], weights
    )
    saved0 = (
        (keep_e0[0], keep_fw0[0]),
        (low_e0, low_fw0),
        (keep_e0[1], keep_fw0[1]),
        (branch_e0, branch_fw0),
    )
    biases0 = (bias_e0, bias_fw0)
    sent0 = sibling_grads(saved0, biases0)
    names = names_of("OW", "x", "c")
    d_rows, columns_x = run(
        functools.partial(row_grad_kernel, edge, names),
        [shaped(worst, d), shaped(1, d, dtype=F32)],
        [*(have[k] for k in names), place, d_edge, d_shared, got_c, logit, vectors],
        flops=one_hot_flops,
        name="row_grad",
        after=(sent0[2],),
        **room(window, 20),
    )
    d_back = exchange(d_rows)

    grad_first, grad_second, grad_bias1 = own_grads(1, saved1, biases1, got1, (), (columns_x,))
    got0 = [swap(v, 1) for v in sent0]
    grad_first, grad_second, grad_bias0 = own_grads(
        0, saved0, biases0, got0, (grad_first, grad_second)
    )

    marks = run(functools.partial(marks_kernel, senders), [shaped(1, d, dtype=F32)], [returned], name="marks")[0]
    row_sums = [columns_x, columns_e0, columns_fw0, columns_ow1, columns_f1, marks]
    columns = run(columns_kernel, [shaped(8, d, dtype=F32)], row_sums)[0]
    columns = run(add_kernel, [shaped(8, d, dtype=F32)], [columns, swap(columns, 1)])[0]
    width = d // lax.axis_size("rep")
    *small, grad_bias, over = run(
        finish_kernel,
        [shaped(n, width, dtype=F32) for n in (1, 2, 2, 2)]
        + [shaped(2, grad_bias0.shape[1], dtype=F32), shaped(1, 128, dtype=F32)],
        [position, columns, swap(columns, 2), grad_bias0, grad_bias1],
        in_specs=[SMEM] + [VMEM] * 4,
    )
    outs = (
        unpack(returned, tokens),
        unpack(d_back, grad_output),
        small[0],
        small[1][None],
        small[2][None],
        grad_first[None],
        grad_bias[None],
        grad_second[None],
        small[3][None],
    )
    return outs, over[0, 0]


def shards(
    tokens, lengths, assign, centroids, ln_gain, ln_bias, w_in, b_in, w_out, b_out, grad_output
):
    experts, reps = lax.axis_size("ex"), lax.axis_size("rep")
    rows_here, d = tokens.shape
    slots = ceil_to(max(2, 5 * rows_here // (4 * experts)) + 1, 8)
    worst = experts * slots
    base = ((lax.axis_index("ex") * reps + lax.axis_index("rep")) * rows_here).astype(jnp.int32).reshape(1)
    target, outgoing = run(
        functools.partial(route_kernel, experts, slots),
        [shaped(1, rows_here, dtype=jnp.int32), shaped(worst, d)],
        [lengths, base, assign.reshape(1, rows_here), tokens],
        in_specs=[SMEM, SMEM, VMEM, VMEM],
        name="route",
        flops=2 * worst * rows_here * d,
    )
    arrived = lax.all_to_all(outgoing, "ex", split_axis=0, concat_axis=0, tiled=True)
    biases = (b_in[0], swap(b_in[0], 1))
    weights = (w_in[0], swap(w_in[0], 1), w_out[0], swap(w_out[0], 1))
    own_vectors = jnp.concatenate([centroids, ln_gain[0], ln_bias[0], b_out[0]], 0)
    own_vectors = jnp.concatenate([own_vectors, outgoing[:1, : own_vectors.shape[1]]], 0)
    vectors = lax.all_gather(own_vectors, "rep", axis=1, tiled=True).astype(F32)
    outgoing_g = run(
        pack_kernel,
        [shaped(worst, d)],
        [target, grad_output],
        flops=2 * worst * rows_here * d,
        after=(vectors,),
    )[0]

    operands = (arrived, outgoing_g, target, tokens, grad_output, vectors, biases, weights)
    most = ceil_to(experts * max(2, 5 * rows_here // (4 * experts)), 16)
    if EDGE + SHARED >= most:
        return expert_group((most, 16), *operands)[0]
    outs, over = expert_group((EDGE, SHARED), *operands)

    def second_pass(*_):
        again = lax.all_to_all(outgoing, "ex", split_axis=0, concat_axis=0, tiled=True)
        return expert_group((most, 16), again, *operands[1:])[0]

    return lax.cond(over > 0.0, second_pass, lambda *kept: kept, *outs)


def solution(mesh):
    rows = P(("ex", "rep"), None)
    in_specs = (
        rows,
        P(),
        rows,
        P("ex", "rep"),
        P("ex", None, "rep"),
        P("ex", None, "rep"),
        P("ex", None, None, "rep"),
        P("ex", None, "rep"),
        P("ex", None, "rep", None),
        P("ex", None, "rep"),
        rows,
    )
    out_specs = (
        rows,
        rows,
        P("ex", "rep"),
        P("ex", None, "rep"),
        P("ex", None, "rep"),
        P("ex", None, None, "rep"),
        P("ex", None, "rep"),
        P("ex", None, "rep", None),
        P("ex", None, "rep"),
    )
    return jax.shard_map(shards, mesh=mesh, in_specs=in_specs, out_specs=out_specs, check_vma=False)
```
